512 devices in a mesh: slab: 16 (over z, y_hi), head: 8 (over y_lo, core), dp: 4 (over x).
Axes of the slice: x: 4, y: 8 (y_hi: 2, y_lo: 4; y = y_hi * 4 + y_lo), z: 8, core: 2. Of those that a mesh axis runs over, the one named last changes fastest.
Arguments:
- q_proj: bfloat16 [4, 6144, 2048], P('dp', ('slab', 'head')), may hold values from -6 to 6
- k_proj: bfloat16 [4, 6144, 2048], P('dp', ('slab', 'head')), may hold values from -6 to 6
- v_proj: bfloat16 [4, 6144, 2048], P('dp', ('slab', 'head')), may hold values from -6 to 6
- grad_out: bfloat16 [4, 6144, 2048], P('dp', ('slab', 'head')), may hold values from -6 to 6
- norm_gains: float32 [2, 128], replicated, may hold values from 0.5 to 1.5
- window_mask: int32 [4, 16, 3], P('dp'), may hold values from 0 to 1, as said below
Outputs:
- attended: bfloat16 [4, 6144, 2048], P('dp', ('slab', 'head'))
- q_grad: bfloat16 [4, 6144, 2048], P('dp', ('slab', 'head'))
- k_grad: bfloat16 [4, 6144, 2048], P('dp', ('slab', 'head'))
- v_grad: bfloat16 [4, 6144, 2048], P('dp', ('slab', 'head'))
- gain_grads: float32 [2, 128], replicated
The draws below stay inside these ranges and needn't reach their ends.
Inputs may be any that keep to these rules, and one draw needn't show every extreme that they name: window_mask[c, t, j] is 0 or 1; the middle slot j = 1 is always 1, and slots that point before the first or after the last of the clip's 16 tiles are 0.
All inputs are finite; a program needn't handle non-finite values.
Results may differ from the reference program's by a relative error of at most 0.0095.
Values may be sent and summed in bfloat16 or wider, within the bound.
A program may use at most 64 MiB of HBM per device.

```python
import jax
import jax.numpy as jnp
from jax import lax

HEADS = 16
HD = 128
TILE = 384
WIN = 3
TILES = 16
TOKENS = 6144
CLIPS = 4


def draw_window_mask(key, part):
    key = jax.random.fold_in(key, 11)
    shape = (CLIPS, TILES, WIN)
    keep = (jax.random.randint(key, shape, 0, 5) < 3).astype(jnp.int32)
    tile = lax.broadcasted_iota(jnp.int32, shape, 1)
    offset = lax.broadcasted_iota(jnp.int32, shape, 2) - WIN // 2
    target = tile + offset
    inside = (target >= 0) & (target < TILES)
    middle = jnp.where(inside, keep, 0)
    return jnp.where(offset == 0, 1, middle).astype(jnp.int32)


def block_scale(rng, extent, pieces, low, top_value):
    def one(position, blocks):
        heights = jax.random.uniform(jax.random.fold_in(jax.random.fold_in(rng, 6), position), (blocks,), jnp.float32, low / len(pieces), top_value / len(pieces))
        return jnp.repeat(jnp.exp(heights), extent[position] // blocks).reshape((-1,) + (1,) * (len(extent) - position - 1))

    loudness = one(*pieces[0])
    for cut in pieces[1:]:
        loudness = loudness * one(*cut)
    return loudness


def noise(key, shape, width, most, split=(), kind=jnp.bfloat16):
    result = width * jax.random.normal(key, shape, jnp.float32)
    if split:
        result = result * block_scale(key, shape, split, -0.22, 0.18)
    return jnp.clip(result, -most, most).astype(kind)


def setup_inputs(seed: int = 0) -> dict:
    seeds = jax.random.split(jax.random.key(seed), 7)
    q_proj = noise(seeds[0], (CLIPS, TOKENS, HEADS * HD), 1.0, 6.0, ((0, 4), (1, 128)))
    k_proj = noise(seeds[1], (CLIPS, TOKENS, HEADS * HD), 1.0, 6.0, ((0, 4), (1, 128)))
    v_proj = noise(seeds[2], (CLIPS, TOKENS, HEADS * HD), 1.0, 6.0, ((0, 4), (1, 128)))
    grad_out = noise(seeds[3], (CLIPS, TOKENS, HEADS * HD), 1.0, 6.0, ((0, 4), (1, 128)))
    norm_gains = jnp.clip(1.0 + 0.1 * jax.random.normal(seeds[4], (2, HD), jnp.float32), 0.5, 1.5)
    window_mask = draw_window_mask(jax.random.fold_in(seeds[6], 71), 0)
    return dict(q_proj=q_proj, k_proj=k_proj, v_proj=v_proj, grad_out=grad_out, norm_gains=norm_gains, window_mask=window_mask)


EPS = 1e-06

def rms_norm(raw, gain):
    values = raw.astype(jnp.float32)
    inverse = lax.rsqrt(lax.optimization_barrier(jnp.mean(values * values, axis=-1, keepdims=True)) + EPS)
    unit = values * inverse
    return (unit, inverse, (unit * gain).astype(jnp.bfloat16))

def norm_backward(unit, inverse, gain, grad):
    inner = grad * gain
    return inverse * (inner - unit * lax.optimization_barrier(jnp.mean(inner * unit, axis=-1, keepdims=True)))

def clip_pass(q_proj, k_proj, v_proj, grad_out, mask, gains):
    shape3 = (TOKENS, HEADS, HD)
    q_unit, q_inv, q_norm = rms_norm(q_proj.reshape(shape3), gains[0])
    k_unit, k_inv, k_norm = rms_norm(k_proj.reshape(shape3), gains[1])
    values = v_proj.reshape(shape3)
    dout = grad_out.reshape(shape3)
    radius = WIN // 2
    margin = radius * TILE
    k_pad = jnp.pad(k_norm, ((margin, margin), (0, 0), (0, 0)))
    v_pad = jnp.pad(values, ((margin, margin), (0, 0), (0, 0)))
    scale = HD ** (-0.5)
    span = WIN * TILE

    def step(carry, tile):
        dk_pad, dv_pad = carry
        start = (tile * TILE).astype(jnp.int32)
        query = lax.dynamic_slice_in_dim(q_norm, start, TILE, 0).astype(jnp.float32)
        dtile = lax.dynamic_slice_in_dim(dout, start, TILE, 0).astype(jnp.float32)
        keys = lax.dynamic_slice_in_dim(k_pad, start, span, 0).astype(jnp.float32)
        vals = lax.dynamic_slice_in_dim(v_pad, start, span, 0).astype(jnp.float32)
        row = lax.dynamic_slice_in_dim(mask, tile.astype(jnp.int32), 1, 0)[0]
        colmask = jnp.repeat(row, TILE) > 0
        score = jnp.einsum('qhd,khd->hqk', query, keys) * scale
        expo = jnp.where(colmask[None, None, :], jnp.exp(score), jnp.float32(0.0))
        denom = lax.optimization_barrier(jnp.sum(expo, axis=-1))
        prob = (expo / denom[..., None]).astype(jnp.bfloat16)
        probf = prob.astype(jnp.float32)
        out_tile = jnp.einsum('hqk,khd->qhd', probf, vals).astype(jnp.bfloat16)
        delta = lax.optimization_barrier(jnp.sum(dtile * out_tile.astype(jnp.float32), axis=-1)).T
        dprob = jnp.einsum('qhd,khd->hqk', dtile, vals)
        dscore = (probf * (dprob - delta[..., None])).astype(jnp.bfloat16).astype(jnp.float32)
        dq_tile = jnp.einsum('hqk,khd->qhd', dscore, keys) * scale
        dk_part = jnp.einsum('hqk,qhd->khd', dscore, query) * scale
        dv_part = jnp.einsum('hqk,qhd->khd', probf, dtile)
        dk_pad = lax.dynamic_update_slice_in_dim(dk_pad, lax.dynamic_slice_in_dim(dk_pad, start, span, 0) + dk_part, start, 0)
        dv_pad = lax.dynamic_update_slice_in_dim(dv_pad, lax.dynamic_slice_in_dim(dv_pad, start, span, 0) + dv_part, start, 0)
        return ((dk_pad, dv_pad), (out_tile, dq_tile))
    zeros = jnp.zeros((TOKENS + 2 * margin, HEADS, HD), jnp.float32)
    (dk_pad, dv_pad), (outs, dqs) = lax.scan(step, (zeros, zeros), jnp.arange(TILES, dtype=jnp.int32))
    attended = outs.reshape(TOKENS, HEADS * HD)
    dq_norm = dqs.reshape(shape3)
    dk_norm = dk_pad[margin:margin + TOKENS]
    v_grad = dv_pad[margin:margin + TOKENS].astype(jnp.bfloat16).reshape(TOKENS, HEADS * HD)
    q_grad = norm_backward(q_unit, q_inv, gains[0], dq_norm).astype(jnp.bfloat16).reshape(TOKENS, HEADS * HD)
    k_grad = norm_backward(k_unit, k_inv, gains[1], dk_norm).astype(jnp.bfloat16).reshape(TOKENS, HEADS * HD)
    gain_part = jnp.stack([lax.optimization_barrier(jnp.sum(dq_norm * q_unit, axis=(0, 1))), lax.optimization_barrier(jnp.sum(dk_norm * k_unit, axis=(0, 1)))])
    return (attended, q_grad, k_grad, v_grad, gain_part)

def reference(q_proj, k_proj, v_proj, grad_out, norm_gains, window_mask):

    def one(items):
        return clip_pass(items[0], items[1], items[2], items[3], items[4], norm_gains)
    attended, q_grad, k_grad, v_grad, parts = lax.map(one, (q_proj, k_proj, v_proj, grad_out, window_mask))
    count = jnp.float32(CLIPS * TOKENS * HEADS)
    gain_grads = lax.optimization_barrier(jnp.sum(parts, axis=0)) / jnp.sqrt(count)
    return (attended, q_grad, k_grad, v_grad, gain_grads)
```

```python
import functools
import math

import jax
import jax.numpy as jnp
from jax import lax
from jax.experimental import pallas as pl
from jax.experimental.pallas import tpu as pltpu
from jax.sharding import PartitionSpec as P

MESH = pl.DeviceIdType.MESH
TILE = 384
HD = 128
EPS = 1e-06
SCALE = HD**-0.5
LOG2E = math.log2(math.e)
LN2 = math.log(2.0)
F32 = jnp.float32
BF16 = jnp.bfloat16


def dot(a, b, dims=((1,), (0,))):
    return lax.dot_general(a, b, (dims, ((), ())), preferred_element_type=F32)


def kernel(
    sizes,
    q_in, k_in, v_in, d_in, gains, mask,
    att_out, qg_out, kg_out, vg_out, gain_out,
    kraw, vbuf, qraw, dbuf,
    knorm, knt, vt, qs,
    kunit, krb, qunit, qrb,
    expo, dsc,
    att, qg, kg, vg,
    halo_out, halo_in,
    gring, gz, gx,
    in_send, in_recv, kv_send, kv_recv, out_send, out_recv, halo_send, halo_recv, g_send, g_recv,
):
    heads, planes, clips, total = sizes
    ring = 2 * heads
    chunk = TILE // heads
    slab = lax.axis_index("slab")
    plane = slab // 2
    side = slab % 2
    me = side * heads + lax.axis_index("head")
    clip = lax.axis_index("dp")

    def ring_id(p):
        return {"slab": 2 * plane + p // heads, "head": p % heads}

    def plane_id(z):
        return {"slab": 2 * z + side}

    def rows(p, base=0):
        return pl.ds(pl.multiple_of(base + p * chunk, 16), chunk)

    def cols(p):
        return pl.ds(pl.multiple_of(p * HD, HD), HD)

    def peer(s):
        off = jnp.where(s % 2 == 1, (s + 1) // 2, ring - s // 2)
        return lax.rem(me + off, ring)

    below = lax.rem(plane + planes - 1, planes)
    above = lax.rem(plane + 1, planes)

    barrier = pltpu.get_barrier_semaphore()

    def greet_ring(s, c):
        pl.semaphore_signal(barrier, inc=1, device_id=ring_id(peer(s)), device_id_type=MESH)
        return c

    def greet_plane(s, c):
        pl.semaphore_signal(
            barrier, inc=1, device_id=plane_id(lax.rem(plane + s, planes)), device_id_type=MESH
        )
        return c

    def greet_clip(s, c):
        pl.semaphore_signal(
            barrier, inc=1, device_id={"dp": lax.rem(clip + s, clips)}, device_id_type=MESH
        )
        return c

    lax.fori_loop(1, ring, greet_ring, 0)
    lax.fori_loop(1, planes, greet_plane, 0)
    lax.fori_loop(1, clips, greet_clip, 0)
    pl.semaphore_wait(barrier, ring - 1 + planes - 1 + clips - 1)

    arrays = ((k_in, kraw, TILE), (v_in, vbuf, TILE), (q_in, qraw, 0), (d_in, dbuf, 0))
    for i, (src, dst, base) in enumerate(arrays):
        pltpu.make_async_copy(
            src.at[0, :, cols(me)], dst.at[rows(me, base), :], in_recv.at[i, side]
        ).start()

    for i, (src, dst, base) in enumerate(arrays):

        def send_in(s, c, i=i, src=src, dst=dst, base=base):
            p = peer(s)
            pltpu.make_async_remote_copy(
                src_ref=src.at[0, :, cols(p)],
                dst_ref=dst.at[rows(me, base), :],
                send_sem=in_send.at[i],
                recv_sem=in_recv.at[i, side],
                device_id=ring_id(p),
                device_id_type=MESH,
            ).start()
            return c

        lax.fori_loop(1, ring, send_in, 0)

    def wait_bytes(ref, sem):
        pltpu.make_async_copy(ref, ref, sem).wait()

    def tile(t):
        return pl.ds(t * TILE, TILE)

    def kv_copy(i, buf, up):
        return pltpu.make_async_remote_copy(
            src_ref=buf.at[tile(2 if up else 1), :],
            dst_ref=buf.at[tile(0 if up else 3), :],
            send_sem=kv_send.at[i, up],
            recv_sem=kv_recv.at[i, up],
            device_id=plane_id(above if up else below),
            device_id_type=MESH,
        )

    kv_copies = []
    for i, buf in ((0, kraw), (1, vbuf)):
        for up in (0, 1):
            wait_bytes(buf.at[tile(1 + up), :], in_recv.at[i, up])
            copy = kv_copy(i, buf, up)
            copy.start()
            kv_copies.append(copy)

    g0 = gains[0:1, :]
    g1 = gains[1:2, :]

    def norm(raw):
        x = raw.astype(F32)
        r = lax.rsqrt(jnp.mean(x * x, axis=-1, keepdims=True) + EPS)
        return x * r, r

    def do_k(t):
        unit, r = norm(kraw[tile(t), :])
        n = unit * g1
        knorm[tile(t), :] = n.astype(BF16)
        knt[:, tile(t)] = n.T.astype(BF16)
        if t in (1, 2):
            kunit[tile(t - 1), :] = unit
            krb[tile(t - 1), :] = jnp.broadcast_to(r, unit.shape)

    def do_v(t):
        vt[:, tile(t)] = vbuf[tile(t), :].astype(F32).T.astype(BF16)

    do_k(1)
    do_k(2)
    do_v(1)
    do_v(2)
    for t, up in ((0, 1), (3, 0)):
        kv_copies[up].wait_recv()
        do_k(t)
        kv_copies[2 + up].wait_recv()
        do_v(t)

    invs = []
    outs = []
    for a in (0, 1):
        wait_bytes(qraw.at[tile(a), :], in_recv.at[2, a])
        unit, r = norm(qraw[tile(a), :])
        qunit[tile(a), :] = unit
        qrb[tile(a), :] = jnp.broadcast_to(r, unit.shape)
        qs[tile(a), :] = (unit * (g0 * (SCALE * LOG2E))).astype(BF16)
    for a in (0, 1):
        den = jnp.zeros((1, TILE), F32)
        for j in range(3):
            on = mask[0, 2 * plane + a, j].astype(F32)
            s = dot(knorm[tile(a + j), :], qs[tile(a), :], ((1,), (1,)))
            e = jnp.exp2(s) * on
            den = den + jnp.sum(e, axis=0, keepdims=True)
            expo[a, tile(j), :] = e.astype(BF16)
        inv = 1.0 / den
        out_t = (dot(vt[:, a * TILE : (a + 3) * TILE], expo[a]) * inv).astype(BF16).astype(F32)
        att[tile(a), :] = out_t.T.astype(BF16)
        invs.append(inv)
        outs.append(out_t)

    def send_out(i, buf, out, a):
        def step(p, c):
            @pl.when(p != me)
            def _():
                pltpu.make_async_remote_copy(
                    src_ref=buf.at[rows(p), :],
                    dst_ref=out.at[0, :, cols(me)],
                    send_sem=out_send.at[i],
                    recv_sem=out_recv.at[i],
                    device_id=ring_id(p),
                    device_id_type=MESH,
                ).start()

            @pl.when(p == me)
            def _():
                pltpu.make_async_copy(buf.at[rows(p), :], out.at[0, :, cols(p)], out_recv.at[i]).start()

            return c

        lax.fori_loop(a * heads, (a + 1) * heads, step, 0)

    send_out(0, att, att_out, 0)
    send_out(0, att, att_out, 1)

    def halo_copy(i, up):
        return pltpu.make_async_remote_copy(
            src_ref=halo_out.at[i, up],
            dst_ref=halo_in.at[i, up],
            send_sem=halo_send.at[i, up],
            recv_sem=halo_recv.at[i, up],
            device_id=plane_id(above if up else below),
            device_id_type=MESH,
        )

    douts = []
    doscs = []
    deltas = []
    halo_copies = {}

    def dscore(a, j):
        dp = dot(vbuf[tile(a + j), :], douts[a])
        dsc[a, tile(j), :] = (expo[a, tile(j), :].astype(F32) * (dp - deltas[a])).astype(BF16)

    for a in (0, 1):
        wait_bytes(dbuf.at[tile(a), :], in_recv.at[3, a])
        dt = dbuf[tile(a), :].astype(F32).T * invs[a]
        dtb = dt.astype(BF16)
        douts.append(dtb)
        doscs.append(dt.T.astype(BF16))
        deltas.append(jnp.sum(dtb.astype(F32) * outs[a], axis=0, keepdims=True))
        j = 2 * a
        halo_out[1, a] = dot(expo[a, tile(j), :], doscs[a]).astype(BF16)
        halo_copies[1, a] = halo_copy(1, a)
        halo_copies[1, a].start()
        dscore(a, j)
        halo_out[0, a] = (dot(dsc[a, tile(j), :], qs[tile(a), :]) * LN2).astype(BF16)
        halo_copies[0, a] = halo_copy(0, a)
        halo_copies[0, a].start()

    def norm_backward(unit, r, gain, grad):
        inner = grad * gain
        return r * (inner - unit * jnp.mean(inner * unit, axis=-1, keepdims=True))

    gain_q = jnp.zeros((1, HD), F32)
    for a in (0, 1):
        for j in range(3):
            if j != 2 * a:
                dscore(a, j)
        dq = dot(knt[:, a * TILE : (a + 3) * TILE], dsc[a]).T * SCALE
        unit = qunit[tile(a), :]
        gain_q = gain_q + jnp.sum(dq * unit, axis=0, keepdims=True)
        qg[tile(a), :] = norm_backward(unit, qrb[tile(a), :], g0, dq).astype(BF16)
        send_out(1, qg, qg_out, a)

    gain_k = jnp.zeros((1, HD), F32)
    for t in (0, 1):
        dv = dot(expo[0, tile(1 + t), :], doscs[0]) + dot(expo[1, tile(t), :], doscs[1])
        halo_copies[1, 1 - t].wait_recv()
        vg[tile(t), :] = (dv + halo_in[1, 1 - t].astype(F32)).astype(BF16)
        send_out(3, vg, vg_out, t)
        dk = dot(dsc[0, tile(1 + t), :], qs[tile(0), :]) + dot(dsc[1, tile(t), :], qs[tile(1), :])
        halo_copies[0, 1 - t].wait_recv()
        dk = dk * LN2 + halo_in[0, 1 - t].astype(F32)
        unit = kunit[tile(t), :]
        gain_k = gain_k + jnp.sum(dk * unit, axis=0, keepdims=True)
        kg[tile(t), :] = norm_backward(unit, krb[tile(t), :], g1, dk).astype(BF16)
        send_out(2, kg, kg_out, t)

    part = jnp.concatenate([gain_q, gain_k, jnp.zeros((6, HD), F32)], axis=0)
    for stage, (buf, here, count, target) in enumerate(
        (
            (gring, me, ring, ring_id),
            (gz, plane, planes, plane_id),
            (gx, clip, clips, lambda x: {"dp": x}),
        )
    ):
        buf[here] = part
        if count > 1:

            def send_gain(s, c, stage=stage, buf=buf, here=here, count=count, target=target):
                pltpu.make_async_remote_copy(
                    src_ref=buf.at[here],
                    dst_ref=buf.at[here],
                    send_sem=g_send.at[stage],
                    recv_sem=g_recv.at[stage],
                    device_id=target(lax.rem(here + s, count)),
                    device_id_type=MESH,
                ).start()
                return c

            lax.fori_loop(1, count, send_gain, 0)
            wait_bytes(buf.at[pl.ds(0, count - 1)], g_recv.at[stage])
        part = jnp.sum(buf[...], axis=0)
    gain_out[...] = part[0:2, :] * (1.0 / math.sqrt(total))

    for i in range(4):
        wait_bytes(att.at[pl.ds(0, 2 * TILE), :], out_recv.at[i])
        wait_bytes(att.at[pl.ds(0, 2 * TILE - chunk), :], out_send.at[i])
        wait_bytes(att.at[pl.ds(0, 2 * TILE - chunk), :], in_send.at[i])
    for copy in kv_copies:
        copy.wait_send()
    for copy in halo_copies.values():
        copy.wait_send()
    for stage, (buf, count) in enumerate(((gring, ring), (gz, planes), (gx, clips))):
        if count > 1:
            wait_bytes(buf.at[pl.ds(0, count - 1)], g_send.at[stage])


def solution(mesh):
    heads = mesh.shape["head"]
    planes = mesh.shape["slab"] // 2
    clips = mesh.shape["dp"]
    ring = 2 * heads
    total = clips * planes * 2 * TILE * ring
    sizes = (heads, planes, clips, total)

    def local(q_proj, k_proj, v_proj, grad_out, norm_gains, window_mask):
        hbm = pl.BlockSpec(memory_space=pltpu.HBM)
        vmem = pl.BlockSpec(memory_space=pltpu.VMEM)
        big = jax.ShapeDtypeStruct(q_proj.shape, BF16)
        dma = pltpu.SemaphoreType.DMA
        return pl.pallas_call(
            functools.partial(kernel, sizes),
            out_shape=(big, big, big, big, jax.ShapeDtypeStruct((2, HD), F32)),
            in_specs=[hbm, hbm, hbm, hbm, vmem, pl.BlockSpec(memory_space=pltpu.SMEM)],
            out_specs=(hbm, hbm, hbm, hbm, vmem),
            scratch_shapes=[
                pltpu.VMEM((4 * TILE, HD), BF16),
                pltpu.VMEM((4 * TILE, HD), BF16),
                pltpu.VMEM((2 * TILE, HD), BF16),
                pltpu.VMEM((2 * TILE, HD), BF16),
                pltpu.VMEM((4 * TILE, HD), BF16),
                pltpu.VMEM((HD, 4 * TILE), BF16),
                pltpu.VMEM((HD, 4 * TILE), BF16),
                pltpu.VMEM((2 * TILE, HD), BF16),
                pltpu.VMEM((2 * TILE, HD), F32),
                pltpu.VMEM((2 * TILE, HD), F32),
                pltpu.VMEM((2 * TILE, HD), F32),
                pltpu.VMEM((2 * TILE, HD), F32),
                pltpu.VMEM((2, 3 * TILE, TILE), BF16),
                pltpu.VMEM((2, 3 * TILE, TILE), BF16),
                pltpu.VMEM((2 * TILE, HD), BF16),
                pltpu.VMEM((2 * TILE, HD), BF16),
                pltpu.VMEM((2 * TILE, HD), BF16),
                pltpu.VMEM((2 * TILE, HD), BF16),
                pltpu.VMEM((2, 2, TILE, HD), BF16),
                pltpu.VMEM((2, 2, TILE, HD), BF16),
                pltpu.VMEM((ring, 8, HD), F32),
                pltpu.VMEM((planes, 8, HD), F32),
                pltpu.VMEM((clips, 8, HD), F32),
                dma((4,)),
                dma((4, 2)),
                dma((2, 2)),
                dma((2, 2)),
                dma((4,)),
                dma((4,)),
                dma((2, 2)),
                dma((2, 2)),
                dma((3,)),
                dma((3,)),
            ],
            compiler_params=pltpu.CompilerParams(
                collective_id=0, has_side_effects=True, vmem_limit_bytes=40 * 1024 * 1024
            ),
        )(q_proj, k_proj, v_proj, grad_out, norm_gains, window_mask)

    tokens = P("dp", ("slab", "head"), None)
    return jax.shard_map(
        local,
        mesh=mesh,
        in_specs=(tokens, tokens, tokens, tokens, P(), P("dp", None, None)),
        out_specs=(tokens, tokens, tokens, tokens, P()),
        check_vma=False,
    )
```

```python
import functools
import math

import jax
import jax.numpy as jnp
from jax import lax
from jax.experimental import pallas as pl
from jax.experimental.pallas import tpu as pltpu
from jax.sharding import PartitionSpec as P

MESH = pl.DeviceIdType.MESH
TILE = 384
HD = 128
EPS = 1e-06
SCALE = HD**-0.5
LOG2E = math.log2(math.e)
LN2 = math.log(2.0)
F32 = jnp.float32
BF16 = jnp.bfloat16


def dot(a, b, dims=((1,), (0,))):
    return lax.dot_general(a, b, (dims, ((), ())), preferred_element_type=F32)


def kernel(
    sizes,
    q_in, k_in, v_in, d_in, gains_in, mask_in,
    att_out, qg_out, kg_out, vg_out, gain_out,
    kraw, vbuf, qraw, dbuf,
    knorm, knt, vt, qs,
    kunit, krb, qunit, qrb,
    expo, dsc,
    att, qg, kg, vg,
    halo_out, halo_in,
    gring, gz, gx, gains, mask,
    small_sem, in_send, in_recv, kv_send, kv_recv, out_send, out_recv, halo_send, halo_recv, g_send, g_recv,
):
    heads, planes, clips, total = sizes
    ring = 2 * heads
    chunk = TILE // heads
    slab = lax.axis_index("slab")
    plane = slab // 2
    side = slab % 2
    me = side * heads + lax.axis_index("head")
    clip = lax.axis_index("dp")

    def ring_id(p):
        return {"slab": 2 * plane + p // heads, "head": p % heads}

    def plane_id(z):
        return {"slab": 2 * z + side}

    def rows(p, base=0):
        return pl.ds(pl.multiple_of(base + p * chunk, 16), chunk)

    def cols(p):
        return pl.ds(pl.multiple_of(p * HD, HD), HD)

    def peer(s):
        off = jnp.where(s % 2 == 1, (s + 1) // 2, ring - s // 2)
        return lax.rem(me + off, ring)

    below = lax.rem(plane + planes - 1, planes)
    above = lax.rem(plane + 1, planes)

    small = (
        pltpu.make_async_copy(gains_in, gains, small_sem.at[0]),
        pltpu.make_async_copy(mask_in, mask, small_sem.at[1]),
    )
    for copy in small:
        copy.start()

    barrier = pltpu.get_barrier_semaphore()

    def greet_ring(s, c):
        pl.semaphore_signal(barrier, inc=1, device_id=ring_id(peer(s)), device_id_type=MESH)
        return c

    def greet_plane(s, c):
        pl.semaphore_signal(
            barrier, inc=1, device_id=plane_id(lax.rem(plane + s, planes)), device_id_type=MESH
        )
        return c

    def greet_clip(s, c):
        pl.semaphore_signal(
            barrier, inc=1, device_id={"dp": lax.rem(clip + s, clips)}, device_id_type=MESH
        )
        return c

    lax.fori_loop(1, ring, greet_ring, 0)
    lax.fori_loop(1, planes, greet_plane, 0)
    lax.fori_loop(1, clips, greet_clip, 0)
    pl.semaphore_wait(barrier, ring - 1 + planes - 1 + clips - 1)

    arrays = ((k_in, kraw, TILE), (v_in, vbuf, TILE), (q_in, qraw, 0), (d_in, dbuf, 0))
    for i, (src, dst, base) in enumerate(arrays):
        pltpu.make_async_copy(
            src.at[0, :, cols(me)], dst.at[rows(me, base), :], in_recv.at[i, side]
        ).start()

    def send_in(i):
        src, dst, base = arrays[i]

        def step(s, c):
            p = peer(s)
            pltpu.make_async_remote_copy(
                src_ref=src.at[0, :, cols(p)],
                dst_ref=dst.at[rows(me, base), :],
                send_sem=in_send.at[i],
                recv_sem=in_recv.at[i, side],
                device_id=ring_id(p),
                device_id_type=MESH,
            ).start()
            return c

        lax.fori_loop(1, ring, step, 0)

    send_in(0)
    send_in(1)

    def wait_bytes(ref, sem):
        pltpu.make_async_copy(ref, ref, sem).wait()

    def tile(t):
        return pl.ds(t * TILE, TILE)

    def kv_copy(i, buf, up):
        return pltpu.make_async_remote_copy(
            src_ref=buf.at[tile(2 if up else 1), :],
            dst_ref=buf.at[tile(0 if up else 3), :],
            send_sem=kv_send.at[i, up],
            recv_sem=kv_recv.at[i, up],
            device_id=plane_id(above if up else below),
            device_id_type=MESH,
        )

    kv_copies = []
    for i, buf in ((0, kraw), (1, vbuf)):
        for up in (0, 1):
            wait_bytes(buf.at[tile(1 + up), :], in_recv.at[i, up])
            copy = kv_copy(i, buf, up)
            copy.start()
            kv_copies.append(copy)
        send_in(2 + i)

    for copy in small:
        copy.wait()
    g0 = gains[0:1, :]
    g1 = gains[1:2, :]

    def norm(raw):
        x = raw.astype(F32)
        r = lax.rsqrt(jnp.mean(x * x, axis=-1, keepdims=True) + EPS)
        return x * r, r

    def do_k(t):
        unit, r = norm(kraw[tile(t), :])
        n = unit * g1
        knorm[tile(t), :] = n.astype(BF16)
        knt[:, tile(t)] = n.T.astype(BF16)
        if t in (1, 2):
            kunit[tile(t - 1), :] = unit
            krb[tile(t - 1), :] = jnp.broadcast_to(r, unit.shape)

    def do_v(t):
        vt[:, tile(t)] = vbuf[tile(t), :].astype(F32).T.astype(BF16)

    do_k(1)
    do_k(2)
    do_v(1)
    do_v(2)
    for t, up in ((0, 1), (3, 0)):
        kv_copies[up].wait_recv()
        do_k(t)
        kv_copies[2 + up].wait_recv()
        do_v(t)

    invs = []
    outs = []
    for a in (0, 1):
        wait_bytes(qraw.at[tile(a), :], in_recv.at[2, a])
        unit, r = norm(qraw[tile(a), :])
        qunit[tile(a), :] = unit
        qrb[tile(a), :] = jnp.broadcast_to(r, unit.shape)
        qs[tile(a), :] = (unit * (g0 * (SCALE * LOG2E))).astype(BF16)
    for a in (0, 1):
        den = jnp.zeros((1, TILE), F32)
        for j in range(3):
            on = mask[j, 0, 2 * plane + a].astype(F32)
            s = dot(knorm[tile(a + j), :], qs[tile(a), :], ((1,), (1,)))
            e = jnp.exp2(s) * on
            den = den + jnp.sum(e, axis=0, keepdims=True)
            expo[a, tile(j), :] = e.astype(BF16)
        inv = 1.0 / den
        out_t = (dot(vt[:, a * TILE : (a + 3) * TILE], expo[a]) * inv).astype(BF16).astype(F32)
        att[tile(a), :] = out_t.T.astype(BF16)
        invs.append(inv)
        outs.append(out_t)

    def send_out(i, buf, out, a):
        def step(s, c):
            p = a * heads + lax.rem(me + s, heads)

            @pl.when(p != me)
            def _():
                pltpu.make_async_remote_copy(
                    src_ref=buf.at[rows(p), :],
                    dst_ref=out.at[0, :, cols(me)],
                    send_sem=out_send.at[i],
                    recv_sem=out_recv.at[i],
                    device_id=ring_id(p),
                    device_id_type=MESH,
                ).start()

            @pl.when(p == me)
            def _():
                pltpu.make_async_copy(buf.at[rows(p), :], out.at[0, :, cols(p)], out_recv.at[i]).start()

            return c

        lax.fori_loop(0, heads, step, 0)

    send_out(0, att, att_out, 0)
    send_out(0, att, att_out, 1)

    def halo_copy(i, up):
        return pltpu.make_async_remote_copy(
            src_ref=halo_out.at[i, up],
            dst_ref=halo_in.at[i, up],
            send_sem=halo_send.at[i, up],
            recv_sem=halo_recv.at[i, up],
            device_id=plane_id(above if up else below),
            device_id_type=MESH,
        )

    douts = []
    doscs = []
    deltas = []
    halo_copies = {}

    def dscore(a, j):
        dp = dot(vbuf[tile(a + j), :], douts[a])
        dsc[a, tile(j), :] = (expo[a, tile(j), :].astype(F32) * (dp - deltas[a])).astype(BF16)

    for a in (0, 1):
        wait_bytes(dbuf.at[tile(a), :], in_recv.at[3, a])
        dt = dbuf[tile(a), :].astype(F32).T * invs[a]
        dtb = dt.astype(BF16)
        douts.append(dtb)
        doscs.append(dt.T.astype(BF16))
        deltas.append(jnp.sum(dtb.astype(F32) * outs[a], axis=0, keepdims=True))
        j = 2 * a
        halo_out[1, a] = dot(expo[a, tile(j), :], doscs[a]).astype(BF16)
        halo_copies[1, a] = halo_copy(1, a)
        halo_copies[1, a].start()
        dscore(a, j)
        halo_out[0, a] = (dot(dsc[a, tile(j), :], qs[tile(a), :]) * LN2).astype(BF16)
        halo_copies[0, a] = halo_copy(0, a)
        halo_copies[0, a].start()

    def norm_backward(unit, r, gain, grad):
        inner = grad * gain
        return r * (inner - unit * jnp.mean(inner * unit, axis=-1, keepdims=True))

    gain_q = jnp.zeros((1, HD), F32)
    for a in (0, 1):
        for j in range(3):
            if j != 2 * a:
                dscore(a, j)
        dq = dot(knt[:, a * TILE : (a + 3) * TILE], dsc[a]).T * SCALE
        unit = qunit[tile(a), :]
        gain_q = gain_q + jnp.sum(dq * unit, axis=0, keepdims=True)
        qg[tile(a), :] = norm_backward(unit, qrb[tile(a), :], g0, dq).astype(BF16)
        send_out(1, qg, qg_out, a)

    gain_k = jnp.zeros((1, HD), F32)
    for t in (0, 1):
        dk = dot(dsc[0, tile(1 + t), :], qs[tile(0), :]) + dot(dsc[1, tile(t), :], qs[tile(1), :])
        halo_copies[0, 1 - t].wait_recv()
        dk = dk * LN2 + halo_in[0, 1 - t].astype(F32)
        unit = kunit[tile(t), :]
        gain_k = gain_k + jnp.sum(dk * unit, axis=0, keepdims=True)
        kg[tile(t), :] = norm_backward(unit, krb[tile(t), :], g1, dk).astype(BF16)

    stages = (
        (gring, me, ring, ring_id),
        (gz, plane, planes, plane_id),
        (gx, clip, clips, lambda x: {"dp": x}),
    )

    def gain_start(stage, part):
        buf, here, count, target = stages[stage]
        buf[here] = part

        def step(s, c):
            pltpu.make_async_remote_copy(
                src_ref=buf.at[here],
                dst_ref=buf.at[here],
                send_sem=g_send.at[stage],
                recv_sem=g_recv.at[stage],
                device_id=target(lax.rem(here + s, count)),
                device_id_type=MESH,
            ).start()
            return c

        lax.fori_loop(1, count, step, 0)

    def gain_end(stage):
        buf, _, count, _ = stages[stage]
        if count > 1:
            wait_bytes(buf.at[pl.ds(0, count - 1)], g_recv.at[stage])
        return jnp.sum(buf[...], axis=0)

    gain_start(0, jnp.concatenate([gain_q, gain_k, jnp.zeros((6, HD), F32)], axis=0))
    for t in (0, 1):
        dv = dot(expo[0, tile(1 + t), :], doscs[0]) + dot(expo[1, tile(t), :], doscs[1])
        halo_copies[1, 1 - t].wait_recv()
        vg[tile(t), :] = (dv + halo_in[1, 1 - t].astype(F32)).astype(BF16)
        send_out(3, vg, vg_out, t)
    gain_start(1, gain_end(0))
    send_out(2, kg, kg_out, 0)
    gain_start(2, gain_end(1))
    send_out(2, kg, kg_out, 1)
    gain_out[...] = gain_end(2)[0:2, :] * (1.0 / math.sqrt(total))

    for i in range(4):
        wait_bytes(att.at[pl.ds(0, 2 * TILE), :], out_recv.at[i])
        wait_bytes(att.at[pl.ds(0, 2 * TILE - chunk), :], out_send.at[i])
        wait_bytes(att.at[pl.ds(0, 2 * TILE - chunk), :], in_send.at[i])
    for copy in kv_copies:
        copy.wait_send()
    for copy in halo_copies.values():
        copy.wait_send()
    for stage, (buf, count) in enumerate(((gring, ring), (gz, planes), (gx, clips))):
        if count > 1:
            wait_bytes(buf.at[pl.ds(0, count - 1)], g_send.at[stage])


def store(*refs):
    sems = refs[10]
    copies = [pltpu.make_async_copy(refs[i], refs[5 + i], sems.at[i]) for i in range(5)]
    for copy in copies:
        copy.start()
    for copy in copies:
        copy.wait()


def solution(mesh):
    heads = mesh.shape["head"]
    planes = mesh.shape["slab"] // 2
    clips = mesh.shape["dp"]
    ring = 2 * heads
    total = clips * planes * 2 * TILE * ring
    sizes = (heads, planes, clips, total)

    def local(q_proj, k_proj, v_proj, grad_out, norm_gains, window_mask):
        hbm = pl.BlockSpec(memory_space=pltpu.HBM)
        vmem = pl.BlockSpec(memory_space=pltpu.VMEM)
        big = jax.ShapeDtypeStruct(q_proj.shape, BF16)
        outs_shape = (big, big, big, big, jax.ShapeDtypeStruct((2, HD), F32))
        landing = tuple(pltpu.VMEM(x.shape, x.dtype) for x in outs_shape)
        operands = (q_proj, k_proj, v_proj, grad_out, norm_gains, jnp.transpose(window_mask, (2, 0, 1)))
        dma = pltpu.SemaphoreType.DMA
        outs = pl.pallas_call(
            functools.partial(kernel, sizes),
            out_shape=landing,
            in_specs=[hbm] * 6,
            out_specs=(vmem,) * 5,
            scratch_shapes=[
                pltpu.VMEM((4 * TILE, HD), BF16),
                pltpu.VMEM((4 * TILE, HD), BF16),
                pltpu.VMEM((2 * TILE, HD), BF16),
                pltpu.VMEM((2 * TILE, HD), BF16),
                pltpu.VMEM((4 * TILE, HD), BF16),
                pltpu.VMEM((HD, 4 * TILE), BF16),
                pltpu.VMEM((HD, 4 * TILE), BF16),
                pltpu.VMEM((2 * TILE, HD), BF16),
                pltpu.VMEM((2 * TILE, HD), F32),
                pltpu.VMEM((2 * TILE, HD), F32),
                pltpu.VMEM((2 * TILE, HD), F32),
                pltpu.VMEM((2 * TILE, HD), F32),
                pltpu.VMEM((2, 3 * TILE, TILE), BF16),
                pltpu.VMEM((2, 3 * TILE, TILE), BF16),
                pltpu.VMEM((2 * TILE, HD), BF16),
                pltpu.VMEM((2 * TILE, HD), BF16),
                pltpu.VMEM((2 * TILE, HD), BF16),
                pltpu.VMEM((2 * TILE, HD), BF16),
                pltpu.VMEM((2, 2, TILE, HD), BF16),
                pltpu.VMEM((2, 2, TILE, HD), BF16),
                pltpu.VMEM((ring, 8, HD), F32),
                pltpu.VMEM((planes, 8, HD), F32),
                pltpu.VMEM((clips, 8, HD), F32),
                pltpu.VMEM((2, HD), F32),
                pltpu.SMEM((3, 1, 2 * planes), jnp.int32),
                dma((2,)),
                dma((4,)),
                dma((4, 2)),
                dma((2, 2)),
                dma((2, 2)),
                dma((4,)),
                dma((4,)),
                dma((2, 2)),
                dma((2, 2)),
                dma((3,)),
                dma((3,)),
            ],
            compiler_params=pltpu.CompilerParams(
                collective_id=0, has_side_effects=True, vmem_limit_bytes=40 * 1024 * 1024
            ),
        )(*(pltpu.with_memory_space_constraint(x, pltpu.HBM) for x in operands))
        return pl.pallas_call(
            store,
            out_shape=outs_shape,
            in_specs=[vmem] * 5,
            out_specs=(hbm,) * 5,
            scratch_shapes=[dma((5,))],
        )(*outs)

    tokens = P("dp", ("slab", "head"), None)
    return jax.shard_map(
        local,
        mesh=mesh,
        in_specs=(tokens, tokens, tokens, tokens, P(), P("dp", None, None)),
        out_specs=(tokens, tokens, tokens, tokens, P()),
        check_vma=False,
    )
```

```python
import functools
import math

import jax
import jax.numpy as jnp
from jax import lax
from jax.experimental import pallas as pl
from jax.experimental.pallas import tpu as pltpu
from jax.sharding import PartitionSpec as P

MESH = pl.DeviceIdType.MESH
TILE = 384
HD = 128
EPS = 1e-06
SCALE = HD**-0.5
LOG2E = math.log2(math.e)
LN2 = math.log(2.0)
F32 = jnp.float32
BF16 = jnp.bfloat16


def dot(a, b, dims=((1,), (0,))):
    return lax.dot_general(a, b, (dims, ((), ())), preferred_element_type=F32)


def kernel(
    sizes,
    q_in, k_in, v_in, d_in, gains_in, mask_in,
    att_out, qg_out, kg_out, vg_out, gain_out,
    kraw, vbuf, qraw, dbuf,
    knorm, knt, vt, qs, qst,
    kunit, krb, qunit, qrb,
    expo, dsc,
    att, qg, kg, vg,
    halo_out, halo_in, den, out_t, dout_t, dout_s, delta,
    gring, gz, gx, gains, mask,
    small_sem, in_send, in_recv, kv_send, kv_recv, out_send, out_recv, halo_send, halo_recv, g_send, g_recv,
):
    heads, planes, clips, total = sizes
    ring = 2 * heads
    chunk = TILE // heads
    slab = lax.axis_index("slab")
    plane = lax.div(slab, 2)
    side = lax.rem(slab, 2)
    me = side * heads + lax.axis_index("head")
    clip = lax.axis_index("dp")

    def ring_id(p):
        return {"slab": 2 * plane + lax.div(p, heads), "head": lax.rem(p, heads)}

    def plane_id(z):
        return {"slab": 2 * z + side}

    def rows(p, base=0):
        return pl.ds(pl.multiple_of(base + p * chunk, 16), chunk)

    def cols(p):
        return pl.ds(pl.multiple_of(p * HD, HD), HD)

    def peer(s):
        half = lax.div(s + 1, 2)
        off = jnp.where(lax.rem(s, 2) == 1, half, ring - half)
        return lax.rem(me + off, ring)

    below = lax.rem(plane + planes - 1, planes)
    above = lax.rem(plane + 1, planes)

    small = (
        pltpu.make_async_copy(gains_in, gains, small_sem.at[0]),
        pltpu.make_async_copy(mask_in, mask, small_sem.at[1]),
    )
    for copy in small:
        copy.start()

    barrier = pltpu.get_barrier_semaphore()

    def greet_ring(s, c):
        pl.semaphore_signal(barrier, inc=1, device_id=ring_id(peer(s)), device_id_type=MESH)
        return c

    def greet_plane(s, c):
        pl.semaphore_signal(
            barrier, inc=1, device_id=plane_id(lax.rem(plane + s, planes)), device_id_type=MESH
        )
        return c

    def greet_clip(s, c):
        pl.semaphore_signal(
            barrier, inc=1, device_id={"dp": lax.rem(clip + s, clips)}, device_id_type=MESH
        )
        return c

    lax.fori_loop(1, ring, greet_ring, 0)
    lax.fori_loop(1, planes, greet_plane, 0)
    lax.fori_loop(1, clips, greet_clip, 0)
    pl.semaphore_wait(barrier, ring - 1 + planes - 1 + clips - 1)

    arrays = ((k_in, kraw, TILE), (q_in, qraw, 0), (v_in, vbuf, TILE), (d_in, dbuf, 0))
    for i, (src, dst, base) in enumerate(arrays):
        pltpu.make_async_copy(
            src.at[0, :, cols(me)], dst.at[rows(me, base), :], in_recv.at[i, side]
        ).start()

    def send_in(i):
        src, dst, base = arrays[i]

        def step(s, c):
            p = peer(s)
            pltpu.make_async_remote_copy(
                src_ref=src.at[0, :, cols(p)],
                dst_ref=dst.at[rows(me, base), :],
                send_sem=in_send.at[i],
                recv_sem=in_recv.at[i, side],
                device_id=ring_id(p),
                device_id_type=MESH,
            ).start()
            return c

        lax.fori_loop(1, ring, step, 0)

    send_in(0)
    send_in(1)

    def wait_bytes(ref, sem):
        pltpu.make_async_copy(ref, ref, sem).wait()

    def tile(t):
        return pl.ds(pl.multiple_of(t * TILE, TILE), TILE)

    def kv_copy(i, up):
        buf = (kraw, vbuf)[i]
        return pltpu.make_async_remote_copy(
            src_ref=buf.at[tile(1 + up), :],
            dst_ref=buf.at[tile(3 - 3 * up), :],
            send_sem=kv_send.at[i, up],
            recv_sem=kv_recv.at[i, up],
            device_id=plane_id(jnp.where(up == 1, above, below)),
            device_id_type=MESH,
        )

    def each(count, body):
        lax.fori_loop(0, count, lambda n, c: (body(n), c)[1], 0)

    def forward_kv(i, arr):
        def step(up):
            wait_bytes((kraw, vbuf)[i].at[tile(1 + up), :], in_recv.at[arr, up])
            kv_copy(i, up).start()

        each(2, step)

    forward_kv(0, 0)
    send_in(2)
    for copy in small:
        copy.wait()

    g0 = gains[0:1, :]
    g1 = gains[1:2, :]

    def norm(raw):
        x = raw.astype(F32)
        r = lax.rsqrt(jnp.mean(x * x, axis=-1, keepdims=True) + EPS)
        return x * r, r

    def do_k(t):
        unit, r = norm(kraw[tile(t), :])
        n = unit * g1
        knorm[tile(t), :] = n.astype(BF16)
        knt[t] = n.T.astype(BF16)
        return unit, r

    def own_k(t):
        unit, r = do_k(t + 1)
        kunit[tile(t), :] = unit
        krb[tile(t), :] = jnp.broadcast_to(r, unit.shape)

    def own_q(a):
        wait_bytes(qraw.at[tile(a), :], in_recv.at[1, a])
        unit, r = norm(qraw[tile(a), :])
        qunit[tile(a), :] = unit
        qrb[tile(a), :] = jnp.broadcast_to(r, unit.shape)
        n = unit * (g0 * (SCALE * LOG2E))
        qs[tile(a), :] = n.astype(BF16)
        qst[a] = n.T.astype(BF16)
        den[a] = jnp.zeros((1, TILE), F32)

    def score(a, j):
        on = mask[j, 0, 2 * plane + a].astype(F32)
        e = jnp.exp2(dot(knorm[tile(a + j), :], qst[a])) * on
        den[a] = den[a] + jnp.sum(e, axis=0, keepdims=True)
        expo[a, tile(j), :] = e.astype(BF16)

    def own_score(n):
        a = lax.div(n, 2)
        score(a, lax.rem(n, 2) + 1 - a)

    def halo_score(u):
        kv_copy(0, 1 - u).wait_recv()
        do_k(3 * u)
        score(u, 2 * u)

    def do_v(t):
        vt[t] = vbuf[tile(t), :].astype(F32).T.astype(BF16)

    def halo_v(u):
        kv_copy(1, 1 - u).wait_recv()
        do_v(3 * u)

    each(2, own_k)
    each(2, own_q)
    send_in(3)
    each(4, own_score)
    each(2, halo_score)
    forward_kv(1, 2)
    each(2, lambda t: do_v(t + 1))
    each(2, halo_v)

    def send_out(i, buf, out, a):
        def step(s, c):
            p = a * heads + lax.rem(me + s, heads)

            @pl.when(p != me)
            def _():
                pltpu.make_async_remote_copy(
                    src_ref=buf.at[rows(p), :],
                    dst_ref=out.at[0, :, cols(me)],
                    send_sem=out_send.at[i],
                    recv_sem=out_recv.at[i],
                    device_id=ring_id(p),
                    device_id_type=MESH,
                ).start()

            @pl.when(p == me)
            def _():
                pltpu.make_async_copy(buf.at[rows(p), :], out.at[0, :, cols(p)], out_recv.at[i]).start()

            return c

        lax.fori_loop(0, heads, step, 0)

    def forward(a):
        total_t = dot(vt[a], expo[a, 0:TILE, :])
        for j in (1, 2):
            total_t = total_t + dot(vt[a + j], expo[a, j * TILE : (j + 1) * TILE, :])
        inv = 1.0 / den[a]
        den[a] = inv
        rounded = (total_t * inv).astype(BF16).astype(F32)
        out_t[a] = rounded
        att[tile(a), :] = rounded.T.astype(BF16)
        send_out(0, att, att_out, a)

    each(2, forward)

    def halo_copy(i, up):
        return pltpu.make_async_remote_copy(
            src_ref=halo_out.at[i, up],
            dst_ref=halo_in.at[i, up],
            send_sem=halo_send.at[i, up],
            recv_sem=halo_recv.at[i, up],
            device_id=plane_id(jnp.where(up == 1, above, below)),
            device_id_type=MESH,
        )

    def dscore(a, j):
        dp = dot(vbuf[tile(a + j), :], dout_t[a])
        dsc[a, tile(j), :] = (expo[a, tile(j), :].astype(F32) * (dp - delta[a])).astype(BF16)

    def norm_backward(unit, r, gain, grad):
        inner = grad * gain
        return r * (inner - unit * jnp.mean(inner * unit, axis=-1, keepdims=True))

    def backward(a, gain):
        wait_bytes(dbuf.at[tile(a), :], in_recv.at[3, a])
        dt = dbuf[tile(a), :].astype(F32).T * den[a]
        dtb = dt.astype(BF16)
        dout_t[a] = dtb
        dout_s[a] = dt.T.astype(BF16)
        delta[a] = jnp.sum(dtb.astype(F32) * out_t[a], axis=0, keepdims=True)
        far = tile(2 * a)
        halo_out[1, a] = dot(expo[a, far, :], dout_s[a]).astype(BF16)
        halo_copy(1, a).start()
        each(3, lambda j: dscore(a, j))
        halo_out[0, a] = (dot(dsc[a, far, :], qs[tile(a), :]) * LN2).astype(BF16)
        halo_copy(0, a).start()
        dq_t = dot(knt[a], dsc[a, 0:TILE, :])
        for j in (1, 2):
            dq_t = dq_t + dot(knt[a + j], dsc[a, j * TILE : (j + 1) * TILE, :])
        dq = dq_t.T * SCALE
        unit = qunit[tile(a), :]
        qg[tile(a), :] = norm_backward(unit, qrb[tile(a), :], g0, dq).astype(BF16)
        send_out(1, qg, qg_out, a)
        return gain + jnp.sum(dq * unit, axis=0, keepdims=True)

    gain_q = lax.fori_loop(0, 2, backward, jnp.zeros((1, HD), F32))

    def finish(t, gain):
        dv = dot(expo[0, tile(1 + t), :], dout_s[0]) + dot(expo[1, tile(t), :], dout_s[1])
        halo_copy(1, 1 - t).wait_recv()
        vg[tile(t), :] = (dv + halo_in[1, 1 - t].astype(F32)).astype(BF16)
        dk = dot(dsc[0, tile(1 + t), :], qs[tile(0), :]) + dot(dsc[1, tile(t), :], qs[tile(1), :])
        halo_copy(0, 1 - t).wait_recv()
        dk = dk * LN2 + halo_in[0, 1 - t].astype(F32)
        unit = kunit[tile(t), :]
        kg[tile(t), :] = norm_backward(unit, krb[tile(t), :], g1, dk).astype(BF16)
        return gain + jnp.sum(dk * unit, axis=0, keepdims=True)

    gain_k = lax.fori_loop(0, 2, finish, jnp.zeros((1, HD), F32))

    stages = (
        (gring, me, ring, ring_id),
        (gz, plane, planes, plane_id),
        (gx, clip, clips, lambda x: {"dp": x}),
    )

    def gain_start(stage, part):
        buf, here, count, target = stages[stage]
        buf[here] = part

        def step(s, c):
            pltpu.make_async_remote_copy(
                src_ref=buf.at[here],
                dst_ref=buf.at[here],
                send_sem=g_send.at[stage],
                recv_sem=g_recv.at[stage],
                device_id=target(lax.rem(here + s, count)),
                device_id_type=MESH,
            ).start()
            return c

        lax.fori_loop(1, count, step, 0)

    def gain_end(stage):
        buf, _, count, _ = stages[stage]
        if count > 1:
            wait_bytes(buf.at[pl.ds(0, count - 1)], g_recv.at[stage])
        return jnp.sum(buf[...], axis=0)

    gain_start(0, jnp.concatenate([gain_q, gain_k, jnp.zeros((6, HD), F32)], axis=0))
    each(2, lambda t: send_out(3, vg, vg_out, t))
    gain_start(1, gain_end(0))
    send_out(2, kg, kg_out, 0)
    gain_start(2, gain_end(1))
    send_out(2, kg, kg_out, 1)
    gain_out[...] = gain_end(2)[0:2, :] * (1.0 / math.sqrt(total))

    for i in range(4):
        wait_bytes(att.at[pl.ds(0, 2 * TILE), :], out_recv.at[i])
        wait_bytes(att.at[pl.ds(0, 2 * TILE - chunk), :], out_send.at[i])
        wait_bytes(att.at[pl.ds(0, 2 * TILE - chunk), :], in_send.at[i])
    for i in range(2):
        for up in range(2):
            kv_copy(i, up).wait_send()
            halo_copy(i, up).wait_send()
    for stage, (buf, count) in enumerate(((gring, ring), (gz, planes), (gx, clips))):
        if count > 1:
            wait_bytes(buf.at[pl.ds(0, count - 1)], g_send.at[stage])


def store(*refs):
    sems = refs[10]
    copies = [pltpu.make_async_copy(refs[i], refs[5 + i], sems.at[i]) for i in range(5)]
    for copy in copies:
        copy.start()
    for copy in copies:
        copy.wait()


def solution(mesh):
    heads = mesh.shape["head"]
    planes = mesh.shape["slab"] // 2
    clips = mesh.shape["dp"]
    ring = 2 * heads
    total = clips * planes * 2 * TILE * ring
    sizes = (heads, planes, clips, total)

    def local(q_proj, k_proj, v_proj, grad_out, norm_gains, window_mask):
        hbm = pl.BlockSpec(memory_space=pltpu.HBM)
        vmem = pl.BlockSpec(memory_space=pltpu.VMEM)
        big = jax.ShapeDtypeStruct(q_proj.shape, BF16)
        outs_shape = (big, big, big, big, jax.ShapeDtypeStruct((2, HD), F32))
        landing = tuple(pltpu.VMEM(x.shape, x.dtype) for x in outs_shape)
        operands = (q_proj, k_proj, v_proj, grad_out, norm_gains, jnp.transpose(window_mask, (2, 0, 1)))
        dma = pltpu.SemaphoreType.DMA
        outs = pl.pallas_call(
            functools.partial(kernel, sizes),
            out_shape=landing,
            in_specs=[hbm] * 6,
            out_specs=(vmem,) * 5,
            scratch_shapes=[
                pltpu.VMEM((4 * TILE, HD), BF16),
                pltpu.VMEM((4 * TILE, HD), BF16),
                pltpu.VMEM((2 * TILE, HD), BF16),
                pltpu.VMEM((2 * TILE, HD), BF16),
                pltpu.VMEM((4 * TILE, HD), BF16),
                pltpu.VMEM((4, HD, TILE), BF16),
                pltpu.VMEM((4, HD, TILE), BF16),
                pltpu.VMEM((2 * TILE, HD), BF16),
                pltpu.VMEM((2, HD, TILE), BF16),
                pltpu.VMEM((2 * TILE, HD), F32),
                pltpu.VMEM((2 * TILE, HD), F32),
                pltpu.VMEM((2 * TILE, HD), F32),
                pltpu.VMEM((2 * TILE, HD), F32),
                pltpu.VMEM((2, 3 * TILE, TILE), BF16),
                pltpu.VMEM((2, 3 * TILE, TILE), BF16),
                pltpu.VMEM((2 * TILE, HD), BF16),
                pltpu.VMEM((2 * TILE, HD), BF16),
                pltpu.VMEM((2 * TILE, HD), BF16),
                pltpu.VMEM((2 * TILE, HD), BF16),
                pltpu.VMEM((2, 2, TILE, HD), BF16),
                pltpu.VMEM((2, 2, TILE, HD), BF16),
                pltpu.VMEM((2, 1, TILE), F32),
                pltpu.VMEM((2, HD, TILE), F32),
                pltpu.VMEM((2, HD, TILE), BF16),
                pltpu.VMEM((2, TILE, HD), BF16),
                pltpu.VMEM((2, 1, TILE), F32),
                pltpu.VMEM((ring, 8, HD), F32),
                pltpu.VMEM((planes, 8, HD), F32),
                pltpu.VMEM((clips, 8, HD), F32),
                pltpu.VMEM((2, HD), F32),
                pltpu.SMEM((3, 1, 2 * planes), jnp.int32),
                dma((2,)),
                dma((4,)),
                dma((4, 2)),
                dma((2, 2)),
                dma((2, 2)),
                dma((4,)),
                dma((4,)),
                dma((2, 2)),
                dma((2, 2)),
                dma((3,)),
                dma((3,)),
            ],
            compiler_params=pltpu.CompilerParams(
                collective_id=0, has_side_effects=True, vmem_limit_bytes=40 * 1024 * 1024
            ),
        )(*(pltpu.with_memory_space_constraint(x, pltpu.HBM) for x in operands))
        return pl.pallas_call(
            store,
            out_shape=outs_shape,
            in_specs=[vmem] * 5,
            out_specs=(hbm,) * 5,
            scratch_shapes=[dma((5,))],
            compiler_params=pltpu.CompilerParams(vmem_limit_bytes=4 * 1024 * 1024),
        )(*(pltpu.with_memory_space_constraint(x, pltpu.VMEM) for x in outs))

    tokens = P("dp", ("slab", "head"), None)
    return jax.shard_map(
        local,
        mesh=mesh,
        in_specs=(tokens, tokens, tokens, tokens, P(), P("dp", None, None)),
        out_specs=(tokens, tokens, tokens, tokens, P()),
        check_vma=False,
    )
```

```python
import functools
import math

import jax
import jax.numpy as jnp
from jax import lax
from jax.experimental import pallas as pl
from jax.experimental.pallas import tpu as pltpu
from jax.sharding import PartitionSpec as P

MESH = pl.DeviceIdType.MESH
TILE = 384
HD = 128
EPS = 1e-06
SCALE = HD**-0.5
LOG2E = math.log2(math.e)
LN2 = math.log(2.0)
F32 = jnp.float32
BF16 = jnp.bfloat16


def dot(a, b, dims=((1,), (0,))):
    return lax.dot_general(a, b, (dims, ((), ())), preferred_element_type=F32)


def kernel(
    sizes,
    q_in, k_in, v_in, d_in, gains_in, mask_in,
    att_out, qg_out, kg_out, vg_out, gain_out,
    kraw, vbuf, qraw, dbuf,
    knorm, knt, vt, qs,
    kunit, krb, qunit, qrb,
    expo, dsc,
    att, qg, kg, vg,
    halo_out, halo_in,
    gring, gz, gx, gains, mask,
    small_sem, in_send, in_recv, kv_send, kv_recv, out_send, out_recv, halo_send, halo_recv, g_send, g_recv,
):
    heads, planes, clips, total = sizes
    ring = 2 * heads
    chunk = TILE // heads
    slab = lax.axis_index("slab")
    plane = lax.div(slab, 2)
    side = lax.rem(slab, 2)
    me = side * heads + lax.axis_index("head")
    clip = lax.axis_index("dp")

    def ring_id(p):
        return {"slab": 2 * plane + lax.div(p, heads), "head": lax.rem(p, heads)}

    def plane_id(z):
        return {"slab": 2 * z + side}

    def rows(p, base=0):
        return pl.ds(pl.multiple_of(base + p * chunk, 16), chunk)

    def cols(p):
        return pl.ds(pl.multiple_of(p * HD, HD), HD)

    def peer(s):
        half = lax.div(s + 1, 2)
        off = jnp.where(lax.rem(s, 2) == 1, half, ring - half)
        return lax.rem(me + off, ring)

    below = lax.rem(plane + planes - 1, planes)
    above = lax.rem(plane + 1, planes)

    small = (
        pltpu.make_async_copy(gains_in, gains, small_sem.at[0]),
        pltpu.make_async_copy(mask_in, mask, small_sem.at[1]),
    )
    for copy in small:
        copy.start()

    barrier = pltpu.get_barrier_semaphore()

    def greet_ring(s, c):
        pl.semaphore_signal(barrier, inc=1, device_id=ring_id(peer(s)), device_id_type=MESH)
        return c

    def greet_plane(s, c):
        pl.semaphore_signal(
            barrier, inc=1, device_id=plane_id(lax.rem(plane + s, planes)), device_id_type=MESH
        )
        return c

    def greet_clip(s, c):
        pl.semaphore_signal(
            barrier, inc=1, device_id={"dp": lax.rem(clip + s, clips)}, device_id_type=MESH
        )
        return c

    lax.fori_loop(1, ring, greet_ring, 0)
    lax.fori_loop(1, planes, greet_plane, 0)
    lax.fori_loop(1, clips, greet_clip, 0)
    pl.semaphore_wait(barrier, ring - 1 + planes - 1 + clips - 1)

    arrays = ((k_in, kraw, TILE), (q_in, qraw, 0), (v_in, vbuf, TILE), (d_in, dbuf, 0))
    for i, (src, dst, base) in enumerate(arrays):
        pltpu.make_async_copy(
            src.at[0, :, cols(me)], dst.at[rows(me, base), :], in_recv.at[i, side]
        ).start()

    def send_in(i):
        src, dst, base = arrays[i]

        def step(s, c):
            p = peer(s)
            pltpu.make_async_remote_copy(
                src_ref=src.at[0, :, cols(p)],
                dst_ref=dst.at[rows(me, base), :],
                send_sem=in_send.at[i],
                recv_sem=in_recv.at[i, side],
                device_id=ring_id(p),
                device_id_type=MESH,
            ).start()
            return c

        lax.fori_loop(1, ring, step, 0)

    send_in(0)
    send_in(1)

    def wait_bytes(ref, sem):
        pltpu.make_async_copy(ref, ref, sem).wait()

    def tile(t):
        return pl.ds(t * TILE, TILE)

    def kv_copy(i, buf, up):
        return pltpu.make_async_remote_copy(
            src_ref=buf.at[tile(2 if up else 1), :],
            dst_ref=buf.at[tile(0 if up else 3), :],
            send_sem=kv_send.at[i, up],
            recv_sem=kv_recv.at[i, up],
            device_id=plane_id(above if up else below),
            device_id_type=MESH,
        )

    kv_copies = {}

    def forward_kv(i, buf, arr):
        for up in (0, 1):
            wait_bytes(buf.at[tile(1 + up), :], in_recv.at[arr, up])
            kv_copies[i, up] = kv_copy(i, buf, up)
            kv_copies[i, up].start()

    forward_kv(0, kraw, 0)
    send_in(2)
    for copy in small:
        copy.wait()

    g0 = gains[0:1, :]
    g1 = gains[1:2, :]

    def norm(raw):
        x = raw.astype(F32)
        r = lax.rsqrt(jnp.mean(x * x, axis=-1, keepdims=True) + EPS)
        return x * r, r

    def do_k(t):
        unit, r = norm(kraw[tile(t), :])
        n = unit * g1
        knorm[tile(t), :] = n.astype(BF16)
        knt[:, tile(t)] = n.T.astype(BF16)
        kunit[tile(t), :] = unit
        if t in (1, 2):
            krb[tile(t - 1), :] = jnp.broadcast_to(r, unit.shape)

    def do_v(t):
        vt[:, tile(t)] = vbuf[tile(t), :].astype(F32).T.astype(BF16)

    do_k(1)
    do_k(2)
    for a in (0, 1):
        wait_bytes(qraw.at[tile(a), :], in_recv.at[1, a])
        unit, r = norm(qraw[tile(a), :])
        qunit[tile(a), :] = unit
        qrb[tile(a), :] = jnp.broadcast_to(r, unit.shape)
        qs[tile(a), :] = (unit * (g0 * (SCALE * LOG2E))).astype(BF16)
    send_in(3)

    dens = [jnp.zeros((1, TILE), F32), jnp.zeros((1, TILE), F32)]

    def score(a, j):
        on = mask[j, 0, 2 * plane + a].astype(F32)
        s = dot(knorm[tile(a + j), :], qs[tile(a), :], ((1,), (1,)))
        e = jnp.exp2(s) * on
        dens[a] = dens[a] + jnp.sum(e, axis=0, keepdims=True)
        expo[a, tile(j), :] = e.astype(BF16)

    score(0, 1)
    score(0, 2)
    score(1, 0)
    score(1, 1)
    kv_copies[0, 1].wait_recv()
    do_k(0)
    score(0, 0)
    kv_copies[0, 0].wait_recv()
    do_k(3)
    score(1, 2)
    forward_kv(1, vbuf, 2)
    do_v(1)
    do_v(2)
    invs = [1.0 / dens[0], 1.0 / dens[1]]
    kv_copies[1, 1].wait_recv()
    do_v(0)
    kv_copies[1, 0].wait_recv()
    do_v(3)
    outs = []
    for a in (0, 1):
        out_t = (dot(vt[:, a * TILE : (a + 3) * TILE], expo[a]) * invs[a]).astype(BF16).astype(F32)
        att[tile(a), :] = out_t.T.astype(BF16)
        outs.append(out_t)

    def send_out(i, buf, out, a):
        def step(s, c):
            p = a * heads + lax.rem(me + s, heads)

            @pl.when(p != me)
            def _():
                pltpu.make_async_remote_copy(
                    src_ref=buf.at[rows(p), :],
                    dst_ref=out.at[0, :, cols(me)],
                    send_sem=out_send.at[i],
                    recv_sem=out_recv.at[i],
                    device_id=ring_id(p),
                    device_id_type=MESH,
                ).start()

            @pl.when(p == me)
            def _():
                pltpu.make_async_copy(buf.at[rows(p), :], out.at[0, :, cols(p)], out_recv.at[i]).start()

            return c

        lax.fori_loop(0, heads, step, 0)

    send_out(0, att, att_out, 0)
    send_out(0, att, att_out, 1)

    def halo_copy(i, up):
        return pltpu.make_async_remote_copy(
            src_ref=halo_out.at[i, up],
            dst_ref=halo_in.at[i, up],
            send_sem=halo_send.at[i, up],
            recv_sem=halo_recv.at[i, up],
            device_id=plane_id(above if up else below),
            device_id_type=MESH,
        )

    douts = []
    doscs = []
    deltas = []
    halo_copies = {}

    def dscore(a, j):
        dp = dot(vbuf[tile(a + j), :], douts[a])
        dsc[a, tile(j), :] = (expo[a, tile(j), :].astype(F32) * (dp - deltas[a])).astype(BF16)

    def norm_backward(unit, r, gain, grad):
        inner = grad * gain
        return r * (inner - unit * jnp.mean(inner * unit, axis=-1, keepdims=True))

    gain_q = jnp.zeros((1, HD), F32)
    gain_k = jnp.zeros((1, HD), F32)
    dqs = []
    for a in (0, 1):
        wait_bytes(dbuf.at[tile(a), :], in_recv.at[3, a])
        dt = dbuf[tile(a), :].astype(F32).T * invs[a]
        dtb = dt.astype(BF16)
        douts.append(dtb)
        doscs.append(dt.T.astype(BF16))
        deltas.append(jnp.sum(dtb.astype(F32) * outs[a], axis=0, keepdims=True))
        j = 2 * a
        halo_out[1, a] = dot(expo[a, tile(j), :], doscs[a]).astype(BF16)
        halo_copies[1, a] = halo_copy(1, a)
        halo_copies[1, a].start()
        dscore(a, j)
        dk = dot(dsc[a, tile(j), :], qs[tile(a), :]) * LN2
        halo_out[0, a] = dk.astype(BF16)
        halo_copies[0, a] = halo_copy(0, a)
        halo_copies[0, a].start()
        gain_k = gain_k + jnp.sum(dk * kunit[tile(3 * a), :], axis=0, keepdims=True)
        dscore(a, 1)
        dscore(a, 2 - j)
        dq = dot(knt[:, a * TILE : (a + 3) * TILE], dsc[a]).T * SCALE
        gain_q = gain_q + jnp.sum(dq * qunit[tile(a), :], axis=0, keepdims=True)
        dqs.append(dq)
    dks = []
    for t in (0, 1):
        dk = dot(dsc[0, tile(1 + t), :], qs[tile(0), :]) + dot(dsc[1, tile(t), :], qs[tile(1), :])
        dk = dk * LN2
        gain_k = gain_k + jnp.sum(dk * kunit[tile(1 + t), :], axis=0, keepdims=True)
        dks.append(dk)

    stages = (
        (gring, me, ring, ring_id),
        (gz, plane, planes, plane_id),
        (gx, clip, clips, lambda x: {"dp": x}),
    )

    def gain_start(stage, part):
        buf, here, count, target = stages[stage]
        buf[here] = part

        def step(s, c):
            pltpu.make_async_remote_copy(
                src_ref=buf.at[here],
                dst_ref=buf.at[here],
                send_sem=g_send.at[stage],
                recv_sem=g_recv.at[stage],
                device_id=target(lax.rem(here + s, count)),
                device_id_type=MESH,
            ).start()
            return c

        lax.fori_loop(1, count, step, 0)

    def gain_end(stage):
        buf, _, count, _ = stages[stage]
        if count > 1:
            wait_bytes(buf.at[pl.ds(0, count - 1)], g_recv.at[stage])
        return jnp.sum(buf[...], axis=0)

    gain_start(0, jnp.concatenate([gain_q, gain_k, jnp.zeros((6, HD), F32)], axis=0))
    for a in (0, 1):
        qg[tile(a), :] = norm_backward(qunit[tile(a), :], qrb[tile(a), :], g0, dqs[a]).astype(BF16)
        send_out(1, qg, qg_out, a)
    for t in (0, 1):
        dv = dot(expo[0, tile(1 + t), :], doscs[0]) + dot(expo[1, tile(t), :], doscs[1])
        halo_copies[1, 1 - t].wait_recv()
        vg[tile(t), :] = (dv + halo_in[1, 1 - t].astype(F32)).astype(BF16)
        halo_copies[0, 1 - t].wait_recv()
        dk = dks[t] + halo_in[0, 1 - t].astype(F32)
        kg[tile(t), :] = norm_backward(kunit[tile(1 + t), :], krb[tile(t), :], g1, dk).astype(BF16)
    gain_start(1, gain_end(0))
    for t in (0, 1):
        send_out(3, vg, vg_out, t)
        send_out(2, kg, kg_out, t)
    gain_start(2, gain_end(1))
    gain_out[...] = gain_end(2)[0:2, :] * (1.0 / math.sqrt(total))

    for i in range(4):
        wait_bytes(att.at[pl.ds(0, 2 * TILE), :], out_recv.at[i])
        wait_bytes(att.at[pl.ds(0, 2 * TILE - chunk), :], out_send.at[i])
        wait_bytes(att.at[pl.ds(0, 2 * TILE - chunk), :], in_send.at[i])
    for copy in kv_copies.values():
        copy.wait_send()
    for copy in halo_copies.values():
        copy.wait_send()
    for stage, (buf, count) in enumerate(((gring, ring), (gz, planes), (gx, clips))):
        if count > 1:
            wait_bytes(buf.at[pl.ds(0, count - 1)], g_send.at[stage])


def store(*refs):
    sems = refs[10]
    copies = [pltpu.make_async_copy(refs[i], refs[5 + i], sems.at[i]) for i in range(5)]
    for copy in copies:
        copy.start()
    for copy in copies:
        copy.wait()


def solution(mesh):
    heads = mesh.shape["head"]
    planes = mesh.shape["slab"] // 2
    clips = mesh.shape["dp"]
    ring = 2 * heads
    total = clips * planes * 2 * TILE * ring
    sizes = (heads, planes, clips, total)

    def local(q_proj, k_proj, v_proj, grad_out, norm_gains, window_mask):
        hbm = pl.BlockSpec(memory_space=pltpu.HBM)
        vmem = pl.BlockSpec(memory_space=pltpu.VMEM)
        big = jax.ShapeDtypeStruct(q_proj.shape, BF16)
        outs_shape = (big, big, big, big, jax.ShapeDtypeStruct((2, HD), F32))
        landing = tuple(pltpu.VMEM(x.shape, x.dtype) for x in outs_shape)
        operands = (q_proj, k_proj, v_proj, grad_out, norm_gains, jnp.transpose(window_mask, (2, 0, 1)))
        dma = pltpu.SemaphoreType.DMA
        outs = pl.pallas_call(
            functools.partial(kernel, sizes),
            out_shape=landing,
            in_specs=[hbm] * 6,
            out_specs=(vmem,) * 5,
            scratch_shapes=[
                pltpu.VMEM((4 * TILE, HD), BF16),
                pltpu.VMEM((4 * TILE, HD), BF16),
                pltpu.VMEM((2 * TILE, HD), BF16),
                pltpu.VMEM((2 * TILE, HD), BF16),
                pltpu.VMEM((4 * TILE, HD), BF16),
                pltpu.VMEM((HD, 4 * TILE), BF16),
                pltpu.VMEM((HD, 4 * TILE), BF16),
                pltpu.VMEM((2 * TILE, HD), BF16),
                pltpu.VMEM((4 * TILE, HD), F32),
                pltpu.VMEM((2 * TILE, HD), F32),
                pltpu.VMEM((2 * TILE, HD), F32),
                pltpu.VMEM((2 * TILE, HD), F32),
                pltpu.VMEM((2, 3 * TILE, TILE), BF16),
                pltpu.VMEM((2, 3 * TILE, TILE), BF16),
                pltpu.VMEM((2 * TILE, HD), BF16),
                pltpu.VMEM((2 * TILE, HD), BF16),
                pltpu.VMEM((2 * TILE, HD), BF16),
                pltpu.VMEM((2 * TILE, HD), BF16),
                pltpu.VMEM((2, 2, TILE, HD), BF16),
                pltpu.VMEM((2, 2, TILE, HD), BF16),
                pltpu.VMEM((ring, 8, HD), F32),
                pltpu.VMEM((planes, 8, HD), F32),
                pltpu.VMEM((clips, 8, HD), F32),
                pltpu.VMEM((2, HD), F32),
                pltpu.SMEM((3, 1, 2 * planes), jnp.int32),
                dma((2,)),
                dma((4,)),
                dma((4, 2)),
                dma((2, 2)),
                dma((2, 2)),
                dma((4,)),
                dma((4,)),
                dma((2, 2)),
                dma((2, 2)),
                dma((3,)),
                dma((3,)),
            ],
            compiler_params=pltpu.CompilerParams(
                collective_id=0, has_side_effects=True, vmem_limit_bytes=40 * 1024 * 1024
            ),
        )(*(pltpu.with_memory_space_constraint(x, pltpu.HBM) for x in operands))
        return pl.pallas_call(
            store,
            out_shape=outs_shape,
            in_specs=[vmem] * 5,
            out_specs=(hbm,) * 5,
            scratch_shapes=[dma((5,))],
            compiler_params=pltpu.CompilerParams(vmem_limit_bytes=4 * 1024 * 1024),
        )(*(pltpu.with_memory_space_constraint(x, pltpu.VMEM) for x in outs))

    tokens = P("dp", ("slab", "head"), None)
    return jax.shard_map(
        local,
        mesh=mesh,
        in_specs=(tokens, tokens, tokens, tokens, P(), P("dp", None, None)),
        out_specs=(tokens, tokens, tokens, tokens, P()),
        check_vma=False,
    )
```

```python
import functools
import math

import jax
import jax.numpy as jnp
from jax import lax
from jax.experimental import pallas as pl
from jax.experimental.pallas import tpu as pltpu
from jax.sharding import PartitionSpec as P

MESH = pl.DeviceIdType.MESH
TILE = 384
HD = 128
EPS = 1e-06
SCALE = HD**-0.5
LOG2E = math.log2(math.e)
LN2 = math.log(2.0)
F32 = jnp.float32
BF16 = jnp.bfloat16


def dot(a, b, dims=((1,), (0,))):
    return lax.dot_general(a, b, (dims, ((), ())), preferred_element_type=F32)


def kernel(
    sizes,
    q_in, k_in, v_in, d_in, gains_in, mask_in,
    att_out, qg_out, kg_out, vg_out, gain_out,
    kraw, vbuf, qraw, dbuf,
    knorm, knt, vt, qs,
    kunit, krb, qunit, qrb,
    expo, dsc,
    att, qg, kg, vg,
    halo_out, halo_in,
    gring, gz, gx, gains, mask,
    small_sem, in_send, in_recv, kv_send, kv_recv, out_send, out_recv, halo_send, halo_recv, g_send, g_recv,
):
    heads, planes, clips, total = sizes
    ring = 2 * heads
    chunk = TILE // heads
    slab = lax.axis_index("slab")
    plane = lax.div(slab, 2)
    side = lax.rem(slab, 2)
    me = side * heads + lax.axis_index("head")
    clip = lax.axis_index("dp")

    def ring_id(p):
        return {"slab": 2 * plane + lax.div(p, heads), "head": lax.rem(p, heads)}

    def plane_id(z):
        return {"slab": 2 * z + side}

    def rows(p, base=0):
        return pl.ds(pl.multiple_of(base + p * chunk, 16), chunk)

    def cols(p):
        return pl.ds(pl.multiple_of(p * HD, HD), HD)

    stride = 7 + 2 * lax.rem(me, 2)

    def peer(s):
        return lax.rem(me + s * stride, ring)

    below = lax.rem(plane + planes - 1, planes)
    above = lax.rem(plane + 1, planes)

    small = (
        pltpu.make_async_copy(gains_in, gains, small_sem.at[0]),
        pltpu.make_async_copy(mask_in, mask, small_sem.at[1]),
    )
    for copy in small:
        copy.start()

    barrier = pltpu.get_barrier_semaphore()

    def greet_ring(s, c):
        pl.semaphore_signal(barrier, inc=1, device_id=ring_id(peer(s)), device_id_type=MESH)
        return c

    def greet_plane(s, c):
        pl.semaphore_signal(
            barrier, inc=1, device_id=plane_id(lax.rem(plane + s, planes)), device_id_type=MESH
        )
        return c

    def greet_clip(s, c):
        pl.semaphore_signal(
            barrier, inc=1, device_id={"dp": lax.rem(clip + s, clips)}, device_id_type=MESH
        )
        return c

    lax.fori_loop(1, ring, greet_ring, 0)
    lax.fori_loop(1, planes, greet_plane, 0)
    lax.fori_loop(1, clips, greet_clip, 0)
    pl.semaphore_wait(barrier, ring - 1 + planes - 1 + clips - 1)

    arrays = ((k_in, kraw, TILE), (v_in, vbuf, TILE), (q_in, qraw, 0), (d_in, dbuf, 0))
    for i, (src, dst, base) in enumerate(arrays):
        pltpu.make_async_copy(
            src.at[0, :, cols(me)], dst.at[rows(me, base), :], in_recv.at[i, side]
        ).start()

    def send_in(i, first=1, end=ring):
        src, dst, base = arrays[i]

        def step(s, c):
            p = peer(s)
            pltpu.make_async_remote_copy(
                src_ref=src.at[0, :, cols(p)],
                dst_ref=dst.at[rows(me, base), :],
                send_sem=in_send.at[i],
                recv_sem=in_recv.at[i, side],
                device_id=ring_id(p),
                device_id_type=MESH,
            ).start()
            return c

        lax.fori_loop(first, end, step, 0)

    send_in(0)
    send_in(1)

    def wait_bytes(ref, sem):
        pltpu.make_async_copy(ref, ref, sem).wait()

    def tile(t):
        return pl.ds(t * TILE, TILE)

    def kv_copy(i, buf, up):
        return pltpu.make_async_remote_copy(
            src_ref=buf.at[tile(2 if up else 1), :],
            dst_ref=buf.at[tile(0 if up else 3), :],
            send_sem=kv_send.at[i, up],
            recv_sem=kv_recv.at[i, up],
            device_id=plane_id(above if up else below),
            device_id_type=MESH,
        )

    kv_copies = {}

    def forward_kv(i, buf, arr):
        for up in (0, 1):
            wait_bytes(buf.at[tile(1 + up), :], in_recv.at[arr, up])
            kv_copies[i, up] = kv_copy(i, buf, up)
            kv_copies[i, up].start()

    forward_kv(0, kraw, 0)
    send_in(2, 1, heads)
    forward_kv(1, vbuf, 1)
    send_in(2, heads, ring)
    send_in(3)
    for copy in small:
        copy.wait()

    g0 = gains[0:1, :]
    g1 = gains[1:2, :]

    def norm(raw):
        x = raw.astype(F32)
        r = lax.rsqrt(jnp.mean(x * x, axis=-1, keepdims=True) + EPS)
        return x * r, r

    def do_k(t):
        unit, r = norm(kraw[tile(t), :])
        n = unit * g1
        knorm[tile(t), :] = n.astype(BF16)
        knt[:, tile(t)] = n.T.astype(BF16)
        kunit[tile(t), :] = unit
        if t in (1, 2):
            krb[tile(t - 1), :] = jnp.broadcast_to(r, unit.shape)

    def do_v(t):
        vt[:, tile(t)] = vbuf[tile(t), :].astype(F32).T.astype(BF16)

    do_k(1)
    do_k(2)
    do_v(1)
    do_v(2)
    for t, up in ((0, 1), (3, 0)):
        kv_copies[0, up].wait_recv()
        do_k(t)
    for t, up in ((0, 1), (3, 0)):
        kv_copies[1, up].wait_recv()
        do_v(t)
    for a in (0, 1):
        wait_bytes(qraw.at[tile(a), :], in_recv.at[2, a])
        unit, r = norm(qraw[tile(a), :])
        qunit[tile(a), :] = unit
        qrb[tile(a), :] = jnp.broadcast_to(r, unit.shape)
        qs[tile(a), :] = (unit * (g0 * (SCALE * LOG2E))).astype(BF16)

    dens = [jnp.zeros((1, TILE), F32), jnp.zeros((1, TILE), F32)]

    def score(a, j):
        on = mask[j, 0, 2 * plane + a].astype(F32)
        s = dot(knorm[tile(a + j), :], qs[tile(a), :], ((1,), (1,)))
        e = jnp.exp2(s) * on
        dens[a] = dens[a] + jnp.sum(e, axis=0, keepdims=True)
        expo[a, tile(j), :] = e.astype(BF16)

    def send_out(i, buf, out, first=1, end=ring):
        def step(s, c):
            p = peer(s)
            pltpu.make_async_remote_copy(
                src_ref=buf.at[rows(p), :],
                dst_ref=out.at[0, :, cols(me)],
                send_sem=out_send.at[i],
                recv_sem=out_recv.at[i],
                device_id=ring_id(p),
                device_id_type=MESH,
            ).start()
            return c

        if first == 1:
            pltpu.make_async_copy(buf.at[rows(me), :], out.at[0, :, cols(me)], out_recv.at[i]).start()
        lax.fori_loop(first, end, step, 0)

    invs = []
    outs = []
    for a in (0, 1):
        for j in range(3):
            score(a, j)
        invs.append(1.0 / dens[a])
        out_t = (dot(vt[:, a * TILE : (a + 3) * TILE], expo[a]) * invs[a]).astype(BF16).astype(F32)
        att[tile(a), :] = out_t.T.astype(BF16)
        outs.append(out_t)
    send_out(0, att, att_out)

    def halo_copy(i, up):
        return pltpu.make_async_remote_copy(
            src_ref=halo_out.at[i, up],
            dst_ref=halo_in.at[i, up],
            send_sem=halo_send.at[i, up],
            recv_sem=halo_recv.at[i, up],
            device_id=plane_id(above if up else below),
            device_id_type=MESH,
        )

    douts = []
    doscs = []
    deltas = []
    halo_copies = {}

    def dscore(a, j):
        dp = dot(vbuf[tile(a + j), :], douts[a])
        dsc[a, tile(j), :] = (expo[a, tile(j), :].astype(F32) * (dp - deltas[a])).astype(BF16)

    def norm_backward(unit, r, gain, grad):
        inner = grad * gain
        return r * (inner - unit * jnp.mean(inner * unit, axis=-1, keepdims=True))

    gain_q = jnp.zeros((1, HD), F32)
    gain_k = jnp.zeros((1, HD), F32)
    dqs = []
    for a in (0, 1):
        wait_bytes(dbuf.at[tile(a), :], in_recv.at[3, a])
        dt = dbuf[tile(a), :].astype(F32).T * invs[a]
        dtb = dt.astype(BF16)
        douts.append(dtb)
        doscs.append(dt.T.astype(BF16))
        deltas.append(jnp.sum(dtb.astype(F32) * outs[a], axis=0, keepdims=True))
        j = 2 * a
        halo_out[1, a] = dot(expo[a, tile(j), :], doscs[a]).astype(BF16)
        halo_copies[1, a] = halo_copy(1, a)
        halo_copies[1, a].start()
        dscore(a, j)
        dk = dot(dsc[a, tile(j), :], qs[tile(a), :]) * LN2
        halo_out[0, a] = dk.astype(BF16)
        halo_copies[0, a] = halo_copy(0, a)
        halo_copies[0, a].start()
        gain_k = gain_k + jnp.sum(dk * kunit[tile(3 * a), :], axis=0, keepdims=True)
        dscore(a, 1)
        dscore(a, 2 - j)
        dq = dot(knt[:, a * TILE : (a + 3) * TILE], dsc[a]).T * SCALE
        gain_q = gain_q + jnp.sum(dq * qunit[tile(a), :], axis=0, keepdims=True)
        dqs.append(dq)
    dks = []
    for t in (0, 1):
        dk = dot(dsc[0, tile(1 + t), :], qs[tile(0), :]) + dot(dsc[1, tile(t), :], qs[tile(1), :])
        dk = dk * LN2
        gain_k = gain_k + jnp.sum(dk * kunit[tile(1 + t), :], axis=0, keepdims=True)
        dks.append(dk)

    stages = (
        (gring, me, ring, ring_id),
        (gz, plane, planes, plane_id),
        (gx, clip, clips, lambda x: {"dp": x}),
    )

    def gain_start(stage, part):
        buf, here, count, target = stages[stage]
        buf[here] = part

        def step(s, c):
            pltpu.make_async_remote_copy(
                src_ref=buf.at[here],
                dst_ref=buf.at[here],
                send_sem=g_send.at[stage],
                recv_sem=g_recv.at[stage],
                device_id=target(lax.rem(here + s, count)),
                device_id_type=MESH,
            ).start()
            return c

        lax.fori_loop(1, count, step, 0)

    def gain_end(stage):
        buf, _, count, _ = stages[stage]
        if count > 1:
            wait_bytes(buf.at[pl.ds(0, count - 1)], g_recv.at[stage])
        return jnp.sum(buf[...], axis=0)

    gain_start(0, jnp.concatenate([gain_q, gain_k, jnp.zeros((6, HD), F32)], axis=0))
    for a in (0, 1):
        qg[tile(a), :] = norm_backward(qunit[tile(a), :], qrb[tile(a), :], g0, dqs[a]).astype(BF16)
    send_out(1, qg, qg_out)
    for t in (0, 1):
        dv = dot(expo[0, tile(1 + t), :], doscs[0]) + dot(expo[1, tile(t), :], doscs[1])
        halo_copies[1, 1 - t].wait_recv()
        vg[tile(t), :] = (dv + halo_in[1, 1 - t].astype(F32)).astype(BF16)
    send_out(3, vg, vg_out)
    gain_start(1, gain_end(0))
    for t in (0, 1):
        halo_copies[0, 1 - t].wait_recv()
        dk = dks[t] + halo_in[0, 1 - t].astype(F32)
        kg[tile(t), :] = norm_backward(kunit[tile(1 + t), :], krb[tile(t), :], g1, dk).astype(BF16)
    send_out(2, kg, kg_out, 1, heads)
    gain_start(2, gain_end(1))
    send_out(2, kg, kg_out, heads, ring)
    gain_out[...] = gain_end(2)[0:2, :] * (1.0 / math.sqrt(total))

    for i in range(4):
        wait_bytes(att.at[pl.ds(0, 2 * TILE), :], out_recv.at[i])
        wait_bytes(att.at[pl.ds(0, 2 * TILE - chunk), :], out_send.at[i])
        wait_bytes(att.at[pl.ds(0, 2 * TILE - chunk), :], in_send.at[i])
    for copy in kv_copies.values():
        copy.wait_send()
    for copy in halo_copies.values():
        copy.wait_send()
    for stage, (buf, count) in enumerate(((gring, ring), (gz, planes), (gx, clips))):
        if count > 1:
            wait_bytes(buf.at[pl.ds(0, count - 1)], g_send.at[stage])


def store(*refs):
    sems = refs[10]
    copies = [pltpu.make_async_copy(refs[i], refs[5 + i], sems.at[i]) for i in range(5)]
    for copy in copies:
        copy.start()
    for copy in copies:
        copy.wait()


def solution(mesh):
    heads = mesh.shape["head"]
    planes = mesh.shape["slab"] // 2
    clips = mesh.shape["dp"]
    ring = 2 * heads
    total = clips * planes * 2 * TILE * ring
    sizes = (heads, planes, clips, total)

    def local(q_proj, k_proj, v_proj, grad_out, norm_gains, window_mask):
        hbm = pl.BlockSpec(memory_space=pltpu.HBM)
        vmem = pl.BlockSpec(memory_space=pltpu.VMEM)
        big = jax.ShapeDtypeStruct(q_proj.shape, BF16)
        outs_shape = (big, big, big, big, jax.ShapeDtypeStruct((2, HD), F32))
        landing = tuple(pltpu.VMEM(x.shape, x.dtype) for x in outs_shape)
        operands = (q_proj, k_proj, v_proj, grad_out, norm_gains, jnp.transpose(window_mask, (2, 0, 1)))
        dma = pltpu.SemaphoreType.DMA
        outs = pl.pallas_call(
            functools.partial(kernel, sizes),
            out_shape=landing,
            in_specs=[hbm] * 6,
            out_specs=(vmem,) * 5,
            scratch_shapes=[
                pltpu.VMEM((4 * TILE, HD), BF16),
                pltpu.VMEM((4 * TILE, HD), BF16),
                pltpu.VMEM((2 * TILE, HD), BF16),
                pltpu.VMEM((2 * TILE, HD), BF16),
                pltpu.VMEM((4 * TILE, HD), BF16),
                pltpu.VMEM((HD, 4 * TILE), BF16),
                pltpu.VMEM((HD, 4 * TILE), BF16),
                pltpu.VMEM((2 * TILE, HD), BF16),
                pltpu.VMEM((4 * TILE, HD), F32),
                pltpu.VMEM((2 * TILE, HD), F32),
                pltpu.VMEM((2 * TILE, HD), F32),
                pltpu.VMEM((2 * TILE, HD), F32),
                pltpu.VMEM((2, 3 * TILE, TILE), BF16),
                pltpu.VMEM((2, 3 * TILE, TILE), BF16),
                pltpu.VMEM((2 * TILE, HD), BF16),
                pltpu.VMEM((2 * TILE, HD), BF16),
                pltpu.VMEM((2 * TILE, HD), BF16),
                pltpu.VMEM((2 * TILE, HD), BF16),
                pltpu.VMEM((2, 2, TILE, HD), BF16),
                pltpu.VMEM((2, 2, TILE, HD), BF16),
                pltpu.VMEM((ring, 8, HD), F32),
                pltpu.VMEM((planes, 8, HD), F32),
                pltpu.VMEM((clips, 8, HD), F32),
                pltpu.VMEM((2, HD), F32),
                pltpu.SMEM((3, 1, 2 * planes), jnp.int32),
                dma((2,)),
                dma((4,)),
                dma((4, 2)),
                dma((2, 2)),
                dma((2, 2)),
                dma((4,)),
                dma((4,)),
                dma((2, 2)),
                dma((2, 2)),
                dma((3,)),
                dma((3,)),
            ],
            compiler_params=pltpu.CompilerParams(
                collective_id=0, has_side_effects=True, vmem_limit_bytes=40 * 1024 * 1024
            ),
        )(*(pltpu.with_memory_space_constraint(x, pltpu.HBM) for x in operands))
        return pl.pallas_call(
            store,
            out_shape=outs_shape,
            in_specs=[vmem] * 5,
            out_specs=(hbm,) * 5,
            scratch_shapes=[dma((5,))],
            compiler_params=pltpu.CompilerParams(vmem_limit_bytes=4 * 1024 * 1024),
        )(*(pltpu.with_memory_space_constraint(x, pltpu.VMEM) for x in outs))

    tokens = P("dp", ("slab", "head"), None)
    return jax.shard_map(
        local,
        mesh=mesh,
        in_specs=(tokens, tokens, tokens, tokens, P(), P("dp", None, None)),
        out_specs=(tokens, tokens, tokens, tokens, P()),
        check_vma=False,
    )
```

```python
import functools
import math

import jax
import jax.numpy as jnp
from jax import lax
from jax.experimental import pallas as pl
from jax.experimental.pallas import tpu as pltpu
from jax.sharding import PartitionSpec as P

MESH = pl.DeviceIdType.MESH
TILE = 384
HD = 128
EPS = 1e-06
SCALE = HD**-0.5
LOG2E = math.log2(math.e)
LN2 = math.log(2.0)
F32 = jnp.float32
BF16 = jnp.bfloat16


def dot(a, b, dims=((1,), (0,))):
    return lax.dot_general(a, b, (dims, ((), ())), preferred_element_type=F32)


def kernel(
    sizes,
    q_in, k_in, v_in, d_in, gains_in, mask_in,
    land, gain_out,
    rx, kh, vh,
    knorm, knt, vt, qs, qst,
    kunit, krb, qunit, qrb,
    expo, dsc, ob, hg_out, hg_in,
    gring, gz, gx, gains, mask,
    small_sem, in_send, in_recv, kv_send, kv_recv, hg_send, hg_recv, out_send, out_recv, g_send, g_recv,
):
    heads, planes, clips, total = sizes
    ring = 2 * heads
    chips = heads
    chunk = TILE // heads
    pair = 2 * HD
    slab = lax.axis_index("slab")
    head = lax.axis_index("head")
    clip = lax.axis_index("dp")
    plane = lax.div(slab, 2)
    side = lax.rem(slab, 2)
    core = lax.rem(head, 2)
    me = side * heads + head
    chip = lax.div(me, 2)
    tile = 2 * plane + core

    def ring_id(p):
        return {"slab": 2 * plane + lax.div(p, heads), "head": lax.rem(p, heads)}

    def plane_id(z):
        return {"slab": 2 * z + side}

    def rows(n):
        return pl.ds(pl.multiple_of(n * chunk, 16), chunk)

    def cols(c):
        return pl.ds(pl.multiple_of(c * pair, pair), pair)

    stride = 3 + 2 * core

    other = head + 1 - 2 * core
    next_plane = lax.rem(plane + planes - 1 + 2 * core, planes)
    near = ({"head": other}, {"slab": 2 * next_plane + side, "head": other})
    slots = (1, 2 - 2 * core, 2 * core)

    small = [
        pltpu.make_async_copy(gains_in, gains, small_sem.at[0]),
        pltpu.make_async_copy(mask_in, mask, small_sem.at[1]),
    ]
    for copy in small:
        copy.start()

    barrier = pltpu.get_barrier_semaphore()

    def greet(target):
        pl.semaphore_signal(barrier, inc=1, device_id=target, device_id_type=MESH)

    def greet_ring(s, c):
        greet(ring_id(lax.rem(me + s, ring)))
        return c

    def greet_plane(s, c):
        greet(plane_id(lax.rem(plane + s, planes)))
        return c

    def greet_clip(s, c):
        greet({"dp": lax.rem(clip + s, clips)})
        return c

    lax.fori_loop(1, ring, greet_ring, 0)
    greet(near[1])
    lax.fori_loop(1, planes, greet_plane, 0)
    lax.fori_loop(1, clips, greet_clip, 0)
    pl.semaphore_wait(barrier, ring + planes - 1 + clips - 1)

    def wait_bytes(ref, sem):
        pltpu.make_async_copy(ref, ref, sem).wait()

    def remote(src, dst, send_sem, recv_sem, target):
        return pltpu.make_async_remote_copy(
            src_ref=src,
            dst_ref=dst,
            send_sem=send_sem,
            recv_sem=recv_sem,
            device_id=target,
            device_id_type=MESH,
        )

    sources = (k_in, v_in, q_in, d_in)

    def send_in(i, first=1, end=chips):
        def block(c):
            return sources[i].at[0, :, cols(c)], rx.at[i, rows(head), :]

        def to(c):
            src, dst = block(c)
            remote(src, dst, in_send.at[i], in_recv.at[i], ring_id(2 * c + side)).start()

        def step(s, carry):
            to(lax.rem(chip + s * stride, chips))
            return carry

        lax.fori_loop(first, end, step, 0)
        if end == chips:

            @pl.when(core != side)
            def _():
                to(chip)

            @pl.when(core == side)
            def _():
                src, dst = block(chip)
                pltpu.make_async_copy(src, dst, in_recv.at[i]).start()

    def wait_in(i):
        wait_bytes(rx.at[i], in_recv.at[i])

    def near_copies(src, dst, send_sem, recv_sem, which=(1, 0)):
        copies = [None, None]
        for n in which:
            copies[n] = remote(src(n), dst(n), send_sem.at[n], recv_sem.at[n], near[n])
            copies[n].start()
        return copies

    send_in(0)
    send_in(1)
    wait_in(0)
    k_copies = near_copies(lambda n: rx.at[0], lambda n: kh.at[n], kv_send.at[0], kv_recv.at[0])
    send_in(2, 1, chips // 2)
    wait_in(1)
    v_copies = near_copies(lambda n: rx.at[1], lambda n: vh.at[n], kv_send.at[1], kv_recv.at[1])
    send_in(2, chips // 2, chips)
    send_in(3)
    for copy in small:
        copy.wait()

    g0 = gains[0:1, :]
    g1 = gains[1:2, :]
    both = tuple((h, slice(h * HD, (h + 1) * HD)) for h in (0, 1))

    def norm(raw):
        x = raw.astype(F32)
        r = lax.rsqrt(jnp.mean(x * x, axis=-1, keepdims=True) + EPS)
        return x * r, r

    def span(slot):
        return slice(slot * TILE, (slot + 1) * TILE)

    def keys(slot):
        return rx.at[0] if slot == 0 else kh.at[slot - 1]

    def vals(slot):
        return rx.at[1] if slot == 0 else vh.at[slot - 1]

    def do_k(slot):
        for h, at in both:
            unit, r = norm(keys(slot)[:, at])
            n = (unit * g1).astype(BF16)
            knorm[h, span(slot), :] = n
            knt[h, :, span(slot)] = n.T
            kunit[h, span(slot), :] = unit
            if slot == 0:
                krb[h] = jnp.broadcast_to(r, unit.shape)

    def do_v(slot):
        for h, at in both:
            vt[h, :, span(slot)] = vals(slot)[:, at].T

    dens = [jnp.zeros((1, TILE), F32), jnp.zeros((1, TILE), F32)]

    def score(slot):
        on = mask[slots[slot], 0, tile].astype(F32)
        for h, _ in both:
            e = jnp.exp2(dot(knorm[h, span(slot), :], qst[h])) * on
            dens[h] = dens[h] + jnp.sum(e, axis=0, keepdims=True)
            expo[h, span(slot), :] = e.astype(BF16)

    do_k(0)
    do_v(0)
    k_copies[0].wait_recv()
    do_k(1)
    k_copies[1].wait_recv()
    do_k(2)
    v_copies[0].wait_recv()
    do_v(1)
    v_copies[1].wait_recv()
    do_v(2)
    wait_in(2)
    for h, at in both:
        unit, r = norm(rx[2, :, at])
        qunit[h] = unit
        qrb[h] = jnp.broadcast_to(r, unit.shape)
        n = (unit * (g0 * (SCALE * LOG2E))).astype(BF16)
        qs[h] = n
        qst[h] = n.T
    for slot in range(3):
        score(slot)
    invs = [1.0 / dens[0], 1.0 / dens[1]]

    def send_out(i, first=1, end=heads):
        def block(n):
            return ob.at[i, rows(n), :], land.at[i, :, cols(chip)]

        def to(n):
            src, dst = block(n)
            remote(src, dst, out_send.at[i], out_recv.at[i], {"slab": tile, "head": n}).start()

        def step(s, carry):
            to(lax.rem(head + s * stride, heads))
            return carry

        lax.fori_loop(first, end, step, 0)
        if end == heads:

            @pl.when(core != side)
            def _():
                to(head)

            @pl.when(core == side)
            def _():
                src, dst = block(head)
                pltpu.make_async_copy(src, dst, out_recv.at[i]).start()

    outs = []
    for h, at in both:
        out_t = (dot(vt[h], expo[h]) * invs[h]).astype(BF16)
        ob[0, :, at] = out_t.T
        outs.append(out_t.astype(F32))
    send_out(0)

    def norm_backward(unit, r, gain, grad):
        inner = grad * gain
        return r * (inner - unit * jnp.mean(inner * unit, axis=-1, keepdims=True))

    douts = []
    doscs = []
    deltas = []

    def dscore(slot):
        for h, at in both:
            dp = dot(vals(slot)[:, at], douts[h])
            dsc[h, span(slot), :] = (expo[h, span(slot), :].astype(F32) * (dp - deltas[h])).astype(BF16)

    wait_in(3)
    for h, at in both:
        dt = rx[3, :, at].T.astype(F32) * invs[h]
        dtb = dt.astype(BF16)
        douts.append(dtb)
        deltas.append(jnp.sum(dtb.astype(F32) * outs[h], axis=0, keepdims=True))

    hg_copies = {}

    def send_near(i, n):
        hg_copies[i, n] = remote(hg_out.at[i, n], hg_in.at[i, n], hg_send.at[i, n], hg_recv.at[i, n], near[n])
        hg_copies[i, n].start()

    gain_k = jnp.zeros((1, HD), F32)
    dks = []
    for slot in (2, 1, 0):
        dscore(slot)
        for h, at in both:
            dk = dot(dsc[h, span(slot), :], qs[h]) * LN2
            gain_k = gain_k + jnp.sum(dk * kunit[h, span(slot), :], axis=0, keepdims=True)
            if slot > 0:
                hg_out[0, slot - 1, :, at] = dk.astype(BF16)
            else:
                dks.append(dk)
        if slot > 0:
            send_near(0, slot - 1)
    gain_q = jnp.zeros((1, HD), F32)
    dqs = []
    for h, at in both:
        dq = dot(knt[h], dsc[h]).T * SCALE
        gain_q = gain_q + jnp.sum(dq * qunit[h], axis=0, keepdims=True)
        dqs.append(dq)

    stages = (
        (gring, me, ring, ring_id),
        (gz, plane, planes, plane_id),
        (gx, clip, clips, lambda x: {"dp": x}),
    )

    def gain_start(which, part):
        buf, here, count, target = stages[which]
        buf[here] = part

        def step(s, c):
            remote(
                buf.at[here], buf.at[here], g_send.at[which], g_recv.at[which], target(lax.rem(here + s, count))
            ).start()
            return c

        lax.fori_loop(1, count, step, 0)

    def gain_end(which):
        buf, _, count, _ = stages[which]
        if count > 1:
            wait_bytes(buf.at[pl.ds(0, count - 1)], g_recv.at[which])
        return jnp.sum(buf[...], axis=0)

    gain_start(0, jnp.concatenate([gain_q, gain_k, jnp.zeros((6, HD), F32)], axis=0))
    for h, at in both:
        doscs.append(douts[h].T)
    for n in (1, 0):
        for h, at in both:
            hg_out[1, n, :, at] = dot(expo[h, span(n + 1), :], doscs[h]).astype(BF16)
        send_near(1, n)
    for h, at in both:
        ob[1, :, at] = norm_backward(qunit[h], qrb[h], g0, dqs[h]).astype(BF16)
    send_out(1)
    hg_copies[0, 0].wait_recv()
    hg_copies[0, 1].wait_recv()
    for h, at in both:
        dk = dks[h] + hg_in[0, 0, :, at].astype(F32) + hg_in[0, 1, :, at].astype(F32)
        ob[3, :, at] = norm_backward(kunit[h, span(0), :], krb[h], g1, dk).astype(BF16)
    gain_start(1, gain_end(0))
    send_out(3)
    hg_copies[1, 0].wait_recv()
    hg_copies[1, 1].wait_recv()
    for h, at in both:
        dv = dot(expo[h, span(0), :], doscs[h])
        ob[2, :, at] = (dv + hg_in[1, 0, :, at].astype(F32) + hg_in[1, 1, :, at].astype(F32)).astype(BF16)
    send_out(2, 1, heads // 2)
    gain_start(2, gain_end(1))
    send_out(2, heads // 2, heads)
    gain_out[...] = gain_end(2)[0:2, :] * (1.0 / math.sqrt(total))

    def wait_sent(count):
        for i in range(4):
            wait_bytes(rx.at[i, pl.ds(0, count * chunk), :], in_send.at[i])
            wait_bytes(ob.at[i, pl.ds(0, count * chunk), :], out_send.at[i])

    for i in range(4):
        wait_bytes(ob.at[i], out_recv.at[i])
    for copy in k_copies + v_copies + list(hg_copies.values()):
        copy.wait_send()
    for which, (buf, _, count, _) in enumerate(stages):
        if count > 1:
            wait_bytes(buf.at[pl.ds(0, count - 1)], g_send.at[which])

    @pl.when(core == side)
    def _():
        wait_sent(heads - 1)

    @pl.when(core != side)
    def _():
        wait_sent(heads)


def store(land, gain, att, qg, vg, kg, gain_out, sems):
    copies = [pltpu.make_async_copy(gain, gain_out, sems.at[4])]
    for i, out in enumerate((att, qg, vg, kg)):
        copies.append(pltpu.make_async_copy(land.at[i], out.at[0], sems.at[i]))
    for copy in copies:
        copy.start()
    for copy in copies:
        copy.wait()


def solution(mesh):
    heads = mesh.shape["head"]
    planes = mesh.shape["slab"] // 2
    clips = mesh.shape["dp"]
    ring = 2 * heads
    chunk = TILE // heads
    total = clips * planes * 2 * TILE * ring
    sizes = (heads, planes, clips, total)

    def local(q_proj, k_proj, v_proj, grad_out, norm_gains, window_mask):
        hbm = pl.BlockSpec(memory_space=pltpu.HBM)
        vmem = pl.BlockSpec(memory_space=pltpu.VMEM)
        big = jax.ShapeDtypeStruct(q_proj.shape, BF16)
        sums = jax.ShapeDtypeStruct((2, HD), F32)
        dma = pltpu.SemaphoreType.DMA
        wide = 2 * HD
        landing = (pltpu.VMEM((4, chunk, ring * HD), BF16), pltpu.VMEM((2, HD), F32))
        operands = (q_proj, k_proj, v_proj, grad_out, norm_gains, jnp.transpose(window_mask, (2, 0, 1)))
        outs = pl.pallas_call(
            functools.partial(kernel, sizes),
            out_shape=landing,
            in_specs=[hbm] * 6,
            out_specs=(vmem,) * 2,
            scratch_shapes=[
                pltpu.VMEM((4, TILE, wide), BF16),
                pltpu.VMEM((2, TILE, wide), BF16),
                pltpu.VMEM((2, TILE, wide), BF16),
                pltpu.VMEM((2, 3 * TILE, HD), BF16),
                pltpu.VMEM((2, HD, 3 * TILE), BF16),
                pltpu.VMEM((2, HD, 3 * TILE), BF16),
                pltpu.VMEM((2, TILE, HD), BF16),
                pltpu.VMEM((2, HD, TILE), BF16),
                pltpu.VMEM((2, 3 * TILE, HD), F32),
                pltpu.VMEM((2, TILE, HD), F32),
                pltpu.VMEM((2, TILE, HD), F32),
                pltpu.VMEM((2, TILE, HD), F32),
                pltpu.VMEM((2, 3 * TILE, TILE), BF16),
                pltpu.VMEM((2, 3 * TILE, TILE), BF16),
                pltpu.VMEM((4, TILE, wide), BF16),
                pltpu.VMEM((2, 2, TILE, wide), BF16),
                pltpu.VMEM((2, 2, TILE, wide), BF16),
                pltpu.VMEM((ring, 8, HD), F32),
                pltpu.VMEM((planes, 8, HD), F32),
                pltpu.VMEM((clips, 8, HD), F32),
                pltpu.VMEM((2, HD), F32),
                pltpu.SMEM((3, 1, 2 * planes), jnp.int32),
                dma((2,)),
                dma((4,)),
                dma((4,)),
                dma((2, 2)),
                dma((2, 2)),
                dma((2, 2)),
                dma((2, 2)),
                dma((4,)),
                dma((4,)),
                dma((3,)),
                dma((3,)),
            ],
            compiler_params=pltpu.CompilerParams(
                collective_id=0, has_side_effects=True, vmem_limit_bytes=40 * 1024 * 1024
            ),
        )(*(pltpu.with_memory_space_constraint(x, pltpu.HBM) for x in operands))
        att, qg, vg, kg, gain = pl.pallas_call(
            store,
            out_shape=(big, big, big, big, sums),
            in_specs=[vmem] * 2,
            out_specs=(hbm,) * 5,
            scratch_shapes=[dma((5,))],
            compiler_params=pltpu.CompilerParams(vmem_limit_bytes=4 * 1024 * 1024),
        )(*(pltpu.with_memory_space_constraint(x, pltpu.VMEM) for x in outs))
        return att, qg, kg, vg, gain

    tokens = P("dp", ("slab", "head"), None)
    return jax.shard_map(
        local,
        mesh=mesh,
        in_specs=(tokens, tokens, tokens, tokens, P(), P("dp", None, None)),
        out_specs=(tokens, tokens, tokens, tokens, P()),
        check_vma=False,
    )
```

```python
import functools
import math

import jax
import jax.numpy as jnp
from jax import lax
from jax.experimental import pallas as pl
from jax.experimental.pallas import tpu as pltpu
from jax.sharding import PartitionSpec as P

MESH = pl.DeviceIdType.MESH
TILE = 384
HD = 128
EPS = 1e-06
SCALE = HD**-0.5
LOG2E = math.log2(math.e)
LN2 = math.log(2.0)
F32 = jnp.float32
BF16 = jnp.bfloat16


def dot(a, b, dims=((1,), (0,))):
    return lax.dot_general(a, b, (dims, ((), ())), preferred_element_type=F32)


def kernel(
    sizes,
    q_in, k_in, v_in, d_in, gains_in, mask_in,
    land, gain_out,
    rx, kh, vh,
    knorm, knt, vt, qs, qst,
    kunit, krb, qunit, qrb,
    expo, dsc, ob, hg_out, hg_in,
    gring, gz, gx, gains, mask,
    small_sem, in_send, in_recv, kv_send, kv_recv, hg_send, hg_recv, out_send, out_recv, g_send, g_recv,
):
    heads, planes, clips, total = sizes
    ring = 2 * heads
    chips = heads
    chunk = TILE // heads
    pair = 2 * HD
    slab = lax.axis_index("slab")
    head = lax.axis_index("head")
    clip = lax.axis_index("dp")
    plane = lax.div(slab, 2)
    side = lax.rem(slab, 2)
    core = lax.rem(head, 2)
    me = side * heads + head
    chip = lax.div(me, 2)
    tile = 2 * plane + core

    def ring_id(p):
        return {"slab": 2 * plane + lax.div(p, heads), "head": lax.rem(p, heads)}

    def plane_id(z):
        return {"slab": 2 * z + side}

    def rows(n):
        return pl.ds(pl.multiple_of(n * chunk, 16), chunk)

    def cols(c):
        return pl.ds(pl.multiple_of(c * pair, pair), pair)

    stride = 3 + 2 * core

    other = head + 1 - 2 * core
    next_plane = lax.rem(plane + planes - 1 + 2 * core, planes)
    near = ({"head": other}, {"slab": 2 * next_plane + side, "head": other})
    slots = (1, 2 - 2 * core, 2 * core)

    small = [
        pltpu.make_async_copy(gains_in, gains, small_sem.at[0]),
        pltpu.make_async_copy(mask_in, mask, small_sem.at[1]),
    ]
    for copy in small:
        copy.start()

    barrier = pltpu.get_barrier_semaphore()

    def greet(target):
        pl.semaphore_signal(barrier, inc=1, device_id=target, device_id_type=MESH)

    def greet_ring(s, c):
        greet(ring_id(lax.rem(me + s, ring)))
        return c

    def greet_plane(s, c):
        greet(plane_id(lax.rem(plane + s, planes)))
        return c

    def greet_clip(s, c):
        greet({"dp": lax.rem(clip + s, clips)})
        return c

    lax.fori_loop(1, ring, greet_ring, 0)
    greet(near[1])
    lax.fori_loop(1, planes, greet_plane, 0)
    lax.fori_loop(1, clips, greet_clip, 0)
    pl.semaphore_wait(barrier, ring + planes - 1 + clips - 1)

    def wait_bytes(ref, sem):
        pltpu.make_async_copy(ref, ref, sem).wait()

    def remote(src, dst, send_sem, recv_sem, target):
        return pltpu.make_async_remote_copy(
            src_ref=src,
            dst_ref=dst,
            send_sem=send_sem,
            recv_sem=recv_sem,
            device_id=target,
            device_id_type=MESH,
        )

    sources = (k_in, v_in, q_in, d_in)

    def send_in(i, first=1, end=chips):
        def block(c):
            return sources[i].at[0, :, cols(c)], rx.at[i, rows(head), :]

        def to(c):
            src, dst = block(c)
            remote(src, dst, in_send.at[i], in_recv.at[i], ring_id(2 * c + side)).start()

        def step(s, carry):
            to(lax.rem(chip + s * stride, chips))
            return carry

        lax.fori_loop(first, end, step, 0)
        if end == chips:

            @pl.when(core != side)
            def _():
                to(chip)

            @pl.when(core == side)
            def _():
                src, dst = block(chip)
                pltpu.make_async_copy(src, dst, in_recv.at[i]).start()

    def wait_in(i):
        wait_bytes(rx.at[i], in_recv.at[i])

    def near_copies(src, dst, send_sem, recv_sem, which=(1, 0)):
        copies = [None, None]
        for n in which:
            copies[n] = remote(src(n), dst(n), send_sem.at[n], recv_sem.at[n], near[n])
            copies[n].start()
        return copies

    send_in(0)
    send_in(1)
    wait_in(0)
    k_copies = near_copies(lambda n: rx.at[0], lambda n: kh.at[n], kv_send.at[0], kv_recv.at[0])
    send_in(2, 1, chips // 2)
    wait_in(1)
    v_copies = near_copies(lambda n: rx.at[1], lambda n: vh.at[n], kv_send.at[1], kv_recv.at[1])
    send_in(2, chips // 2, chips)
    send_in(3)
    for copy in small:
        copy.wait()

    g0 = gains[0:1, :]
    g1 = gains[1:2, :]
    both = tuple((h, slice(h * HD, (h + 1) * HD)) for h in (0, 1))

    def norm(raw):
        x = raw.astype(F32)
        r = lax.rsqrt(jnp.mean(x * x, axis=-1, keepdims=True) + EPS)
        return x * r, r

    def span(slot):
        return slice(slot * TILE, (slot + 1) * TILE)

    def keys(slot):
        return rx.at[0] if slot == 0 else kh.at[slot - 1]

    def vals(slot):
        return rx.at[1] if slot == 0 else vh.at[slot - 1]

    def do_k(slot):
        for h, at in both:
            unit, r = norm(keys(slot)[:, at])
            n = (unit * g1).astype(BF16)
            knorm[h, span(slot), :] = n
            knt[h, :, span(slot)] = n.T
            kunit[h, span(slot), :] = unit
            if slot == 0:
                krb[h] = jnp.broadcast_to(r, unit.shape)

    def do_v(slot):
        for h, at in both:
            vt[h, :, span(slot)] = vals(slot)[:, at].T

    dens = [jnp.zeros((1, TILE), F32), jnp.zeros((1, TILE), F32)]

    def score(slot):
        on = mask[slots[slot], 0, tile].astype(F32)
        for h, _ in both:
            e = jnp.exp2(dot(knorm[h, span(slot), :], qst[h])) * on
            dens[h] = dens[h] + jnp.sum(e, axis=0, keepdims=True)
            expo[h, span(slot), :] = e.astype(BF16)

    do_k(0)
    do_v(0)
    k_copies[0].wait_recv()
    do_k(1)
    k_copies[1].wait_recv()
    do_k(2)
    v_copies[0].wait_recv()
    do_v(1)
    v_copies[1].wait_recv()
    do_v(2)
    wait_in(2)
    for h, at in both:
        unit, r = norm(rx[2, :, at])
        qunit[h] = unit
        qrb[h] = jnp.broadcast_to(r, unit.shape)
        n = (unit * (g0 * (SCALE * LOG2E))).astype(BF16)
        qs[h] = n
        qst[h] = n.T
    for slot in range(3):
        score(slot)
    invs = [1.0 / dens[0], 1.0 / dens[1]]

    def send_out(i, first=1, end=heads):
        def block(n):
            return ob.at[i, rows(n), :], land.at[i, chip]

        def to(n):
            src, dst = block(n)
            remote(src, dst, out_send.at[i], out_recv.at[i], {"slab": tile, "head": n}).start()

        def step(s, carry):
            to(lax.rem(head + s * stride, heads))
            return carry

        lax.fori_loop(first, end, step, 0)
        if end == heads:

            @pl.when(core != side)
            def _():
                to(head)

            @pl.when(core == side)
            def _():
                src, dst = block(head)
                pltpu.make_async_copy(src, dst, out_recv.at[i]).start()

    outs = []
    for h, at in both:
        out_t = (dot(vt[h], expo[h]) * invs[h]).astype(BF16)
        ob[0, :, at] = out_t.T
        outs.append(out_t.astype(F32))
    send_out(0)

    def norm_backward(unit, r, gain, grad):
        inner = grad * gain
        return r * (inner - unit * jnp.mean(inner * unit, axis=-1, keepdims=True))

    douts = []
    doscs = []
    deltas = []

    def dscore(slot):
        for h, at in both:
            dp = dot(vals(slot)[:, at], douts[h])
            dsc[h, span(slot), :] = (expo[h, span(slot), :].astype(F32) * (dp - deltas[h])).astype(BF16)

    wait_in(3)
    for h, at in both:
        dt = rx[3, :, at].T.astype(F32) * invs[h]
        dtb = dt.astype(BF16)
        douts.append(dtb)
        deltas.append(jnp.sum(dtb.astype(F32) * outs[h], axis=0, keepdims=True))

    hg_copies = {}

    def send_near(i, n):
        hg_copies[i, n] = remote(hg_out.at[i, n], hg_in.at[i, n], hg_send.at[i, n], hg_recv.at[i, n], near[n])
        hg_copies[i, n].start()

    gain_k = jnp.zeros((1, HD), F32)
    dks = []
    for slot in (2, 1, 0):
        dscore(slot)
        for h, at in both:
            dk = dot(dsc[h, span(slot), :], qs[h]) * LN2
            gain_k = gain_k + jnp.sum(dk * kunit[h, span(slot), :], axis=0, keepdims=True)
            if slot > 0:
                hg_out[0, slot - 1, :, at] = dk.astype(BF16)
            else:
                dks.append(dk)
        if slot > 0:
            send_near(0, slot - 1)
    gain_q = jnp.zeros((1, HD), F32)
    dqs = []
    for h, at in both:
        dq = dot(knt[h], dsc[h]).T * SCALE
        gain_q = gain_q + jnp.sum(dq * qunit[h], axis=0, keepdims=True)
        dqs.append(dq)

    stages = (
        (gring, me, ring, ring_id),
        (gz, plane, planes, plane_id),
        (gx, clip, clips, lambda x: {"dp": x}),
    )

    def gain_start(which, part):
        buf, here, count, target = stages[which]
        buf[here] = part

        def step(s, c):
            remote(
                buf.at[here], buf.at[here], g_send.at[which], g_recv.at[which], target(lax.rem(here + s, count))
            ).start()
            return c

        lax.fori_loop(1, count, step, 0)

    def gain_end(which):
        buf, _, count, _ = stages[which]
        if count > 1:
            wait_bytes(buf.at[pl.ds(0, count - 1)], g_recv.at[which])
        return jnp.sum(buf[...], axis=0)

    gain_start(0, jnp.concatenate([gain_q, gain_k, jnp.zeros((6, HD), F32)], axis=0))
    for h, at in both:
        doscs.append(douts[h].T)
    for n in (1, 0):
        for h, at in both:
            hg_out[1, n, :, at] = dot(expo[h, span(n + 1), :], doscs[h]).astype(BF16)
        send_near(1, n)
    for h, at in both:
        ob[1, :, at] = norm_backward(qunit[h], qrb[h], g0, dqs[h]).astype(BF16)
    send_out(1)
    hg_copies[0, 0].wait_recv()
    hg_copies[0, 1].wait_recv()
    for h, at in both:
        dk = dks[h] + hg_in[0, 0, :, at].astype(F32) + hg_in[0, 1, :, at].astype(F32)
        ob[3, :, at] = norm_backward(kunit[h, span(0), :], krb[h], g1, dk).astype(BF16)
    gain_start(1, gain_end(0))
    send_out(3)
    hg_copies[1, 0].wait_recv()
    hg_copies[1, 1].wait_recv()
    for h, at in both:
        dv = dot(expo[h, span(0), :], doscs[h])
        ob[2, :, at] = (dv + hg_in[1, 0, :, at].astype(F32) + hg_in[1, 1, :, at].astype(F32)).astype(BF16)
    send_out(2, 1, heads // 2)
    gain_start(2, gain_end(1))
    send_out(2, heads // 2, heads)
    gain_out[...] = gain_end(2)[0:2, :] * (1.0 / math.sqrt(total))

    def wait_sent(count):
        for i in range(4):
            wait_bytes(rx.at[i, pl.ds(0, count * chunk), :], in_send.at[i])
            wait_bytes(ob.at[i, pl.ds(0, count * chunk), :], out_send.at[i])

    for i in range(4):
        wait_bytes(ob.at[i], out_recv.at[i])
    for copy in k_copies + v_copies + list(hg_copies.values()):
        copy.wait_send()
    for which, (buf, _, count, _) in enumerate(stages):
        if count > 1:
            wait_bytes(buf.at[pl.ds(0, count - 1)], g_send.at[which])

    @pl.when(core == side)
    def _():
        wait_sent(heads - 1)

    @pl.when(core != side)
    def _():
        wait_sent(heads)


def store(land, gain, att, qg, vg, kg, gain_out, sems):
    copies = [pltpu.make_async_copy(gain, gain_out, sems.at[4, 0])]
    width = land.shape[3]
    for i, out in enumerate((att, qg, vg, kg)):
        for c in range(land.shape[1]):
            copies.append(
                pltpu.make_async_copy(
                    land.at[i, c], out.at[0, :, c * width : (c + 1) * width], sems.at[i, c]
                )
            )
    for copy in copies:
        copy.start()
    for copy in copies:
        copy.wait()


def solution(mesh):
    heads = mesh.shape["head"]
    planes = mesh.shape["slab"] // 2
    clips = mesh.shape["dp"]
    ring = 2 * heads
    chunk = TILE // heads
    total = clips * planes * 2 * TILE * ring
    sizes = (heads, planes, clips, total)

    def local(q_proj, k_proj, v_proj, grad_out, norm_gains, window_mask):
        hbm = pl.BlockSpec(memory_space=pltpu.HBM)
        vmem = pl.BlockSpec(memory_space=pltpu.VMEM)
        big = jax.ShapeDtypeStruct(q_proj.shape, BF16)
        sums = jax.ShapeDtypeStruct((2, HD), F32)
        dma = pltpu.SemaphoreType.DMA
        wide = 2 * HD
        landing = (pltpu.VMEM((4, heads, chunk, wide), BF16), pltpu.VMEM((2, HD), F32))
        operands = (q_proj, k_proj, v_proj, grad_out, norm_gains, jnp.transpose(window_mask, (2, 0, 1)))
        outs = pl.pallas_call(
            functools.partial(kernel, sizes),
            out_shape=landing,
            in_specs=[hbm] * 6,
            out_specs=(vmem,) * 2,
            scratch_shapes=[
                pltpu.VMEM((4, TILE, wide), BF16),
                pltpu.VMEM((2, TILE, wide), BF16),
                pltpu.VMEM((2, TILE, wide), BF16),
                pltpu.VMEM((2, 3 * TILE, HD), BF16),
                pltpu.VMEM((2, HD, 3 * TILE), BF16),
                pltpu.VMEM((2, HD, 3 * TILE), BF16),
                pltpu.VMEM((2, TILE, HD), BF16),
                pltpu.VMEM((2, HD, TILE), BF16),
                pltpu.VMEM((2, 3 * TILE, HD), F32),
                pltpu.VMEM((2, TILE, HD), F32),
                pltpu.VMEM((2, TILE, HD), F32),
                pltpu.VMEM((2, TILE, HD), F32),
                pltpu.VMEM((2, 3 * TILE, TILE), BF16),
                pltpu.VMEM((2, 3 * TILE, TILE), BF16),
                pltpu.VMEM((4, TILE, wide), BF16),
                pltpu.VMEM((2, 2, TILE, wide), BF16),
                pltpu.VMEM((2, 2, TILE, wide), BF16),
                pltpu.VMEM((ring, 8, HD), F32),
                pltpu.VMEM((planes, 8, HD), F32),
                pltpu.VMEM((clips, 8, HD), F32),
                pltpu.VMEM((2, HD), F32),
                pltpu.SMEM((3, 1, 2 * planes), jnp.int32),
                dma((2,)),
                dma((4,)),
                dma((4,)),
                dma((2, 2)),
                dma((2, 2)),
                dma((2, 2)),
                dma((2, 2)),
                dma((4,)),
                dma((4,)),
                dma((3,)),
                dma((3,)),
            ],
            compiler_params=pltpu.CompilerParams(
                collective_id=0, has_side_effects=True, vmem_limit_bytes=40 * 1024 * 1024
            ),
        )(*(pltpu.with_memory_space_constraint(x, pltpu.HBM) for x in operands))
        att, qg, vg, kg, gain = pl.pallas_call(
            store,
            out_shape=(big, big, big, big, sums),
            in_specs=[vmem] * 2,
            out_specs=(hbm,) * 5,
            scratch_shapes=[dma((5, heads))],
            compiler_params=pltpu.CompilerParams(vmem_limit_bytes=4 * 1024 * 1024),
        )(*(pltpu.with_memory_space_constraint(x, pltpu.VMEM) for x in outs))
        return att, qg, kg, vg, gain

    tokens = P("dp", ("slab", "head"), None)
    return jax.shard_map(
        local,
        mesh=mesh,
        in_specs=(tokens, tokens, tokens, tokens, P(), P("dp", None, None)),
        out_specs=(tokens, tokens, tokens, tokens, P()),
        check_vma=False,
    )
```

```python
import functools
import math

import jax
import jax.numpy as jnp
from jax import lax
from jax.experimental import pallas as pl
from jax.experimental.pallas import tpu as pltpu
from jax.sharding import PartitionSpec as P

MESH = pl.DeviceIdType.MESH
TILE = 384
HD = 128
EPS = 1e-06
SCALE = HD**-0.5
LOG2E = math.log2(math.e)
LN2 = math.log(2.0)
F32 = jnp.float32
BF16 = jnp.bfloat16


def dot(a, b, dims=((1,), (0,))):
    return lax.dot_general(a, b, (dims, ((), ())), preferred_element_type=F32)


def kernel(
    sizes,
    q_in, k_in, v_in, d_in, gains_in, mask_in,
    land, gain_out,
    rx, kh, vh,
    knorm, knt, vt, qs, qst,
    kunit, krb, qunit, qrb,
    expo, dsc, ob, hg_out, hg_in,
    gring, gz, gx, gains, mask,
    small_sem, in_send, in_recv, kv_send, kv_recv, hg_send, hg_recv, out_send, out_recv, g_send, g_recv,
):
    heads, planes, clips, total = sizes
    ring = 2 * heads
    chips = heads
    chunk = TILE // heads
    pair = 2 * HD
    slab = lax.axis_index("slab")
    head = lax.axis_index("head")
    clip = lax.axis_index("dp")
    plane = lax.div(slab, 2)
    side = lax.rem(slab, 2)
    core = lax.rem(head, 2)
    me = side * heads + head
    chip = lax.div(me, 2)
    tile = 2 * plane + core

    def ring_id(p):
        return {"slab": 2 * plane + lax.div(p, heads), "head": lax.rem(p, heads)}

    def plane_id(z):
        return {"slab": 2 * z + side}

    def rows(n):
        return pl.ds(pl.multiple_of(n * chunk, 16), chunk)

    def cols(c):
        return pl.ds(pl.multiple_of(c * pair, pair), pair)

    stride = 3 + 2 * core

    other = head + 1 - 2 * core
    next_plane = lax.rem(plane + planes - 1 + 2 * core, planes)
    near = ({"head": other}, {"slab": 2 * next_plane + side, "head": other})
    slots = (1, 2 - 2 * core, 2 * core)

    small = [
        pltpu.make_async_copy(gains_in, gains, small_sem.at[0]),
        pltpu.make_async_copy(mask_in, mask, small_sem.at[1]),
    ]
    for copy in small:
        copy.start()

    barrier = pltpu.get_barrier_semaphore()

    def greet(target):
        pl.semaphore_signal(barrier, inc=1, device_id=target, device_id_type=MESH)

    def greet_ring(s, c):
        greet(ring_id(lax.rem(me + s, ring)))
        return c

    def greet_plane(s, c):
        greet(plane_id(lax.rem(plane + s, planes)))
        return c

    def greet_clip(s, c):
        greet({"dp": lax.rem(clip + s, clips)})
        return c

    lax.fori_loop(1, ring, greet_ring, 0)
    greet(near[1])
    lax.fori_loop(1, planes, greet_plane, 0)
    lax.fori_loop(1, clips, greet_clip, 0)
    pl.semaphore_wait(barrier, ring + planes - 1 + clips - 1)

    def wait_bytes(ref, sem):
        pltpu.make_async_copy(ref, ref, sem).wait()

    def remote(src, dst, send_sem, recv_sem, target):
        return pltpu.make_async_remote_copy(
            src_ref=src,
            dst_ref=dst,
            send_sem=send_sem,
            recv_sem=recv_sem,
            device_id=target,
            device_id_type=MESH,
        )

    sources = (k_in, v_in, q_in, d_in)

    def send_in(i, first=1, end=chips):
        def block(c):
            return sources[i].at[0, :, cols(c)], rx.at[i, rows(head), :]

        def to(c):
            src, dst = block(c)
            remote(src, dst, in_send.at[i], in_recv.at[i], ring_id(2 * c + side)).start()

        def step(s, carry):
            to(lax.rem(chip + s * stride, chips))
            return carry

        lax.fori_loop(first, end, step, 0)
        if end == chips:

            @pl.when(core != side)
            def _():
                to(chip)

            @pl.when(core == side)
            def _():
                src, dst = block(chip)
                pltpu.make_async_copy(src, dst, in_recv.at[i]).start()

    def wait_in(i):
        wait_bytes(rx.at[i], in_recv.at[i])

    def near_copies(src, dst, send_sem, recv_sem, which=(1, 0)):
        copies = [None, None]
        for n in which:
            copies[n] = remote(src(n), dst(n), send_sem.at[n], recv_sem.at[n], near[n])
            copies[n].start()
        return copies

    send_in(0)
    send_in(1)
    wait_in(0)
    k_copies = near_copies(lambda n: rx.at[0], lambda n: kh.at[n], kv_send.at[0], kv_recv.at[0])
    send_in(2, 1, chips // 2)
    wait_in(1)
    v_copies = near_copies(lambda n: rx.at[1], lambda n: vh.at[n], kv_send.at[1], kv_recv.at[1])
    send_in(2, chips // 2, chips)
    send_in(3)
    for copy in small:
        copy.wait()

    g0 = gains[0:1, :]
    g1 = gains[1:2, :]
    both = tuple((h, slice(h * HD, (h + 1) * HD)) for h in (0, 1))

    def norm(raw):
        x = raw.astype(F32)
        r = lax.rsqrt(jnp.mean(x * x, axis=-1, keepdims=True) + EPS)
        return x * r, r

    def span(slot):
        return slice(slot * TILE, (slot + 1) * TILE)

    def keys(slot):
        return rx.at[0] if slot == 0 else kh.at[slot - 1]

    def vals(slot):
        return rx.at[1] if slot == 0 else vh.at[slot - 1]

    def do_k(slot):
        for h, at in both:
            unit, r = norm(keys(slot)[:, at])
            n = (unit * g1).astype(BF16)
            knorm[h, span(slot), :] = n
            knt[h, :, span(slot)] = n.T
            kunit[h, span(slot), :] = unit
            if slot == 0:
                krb[h] = jnp.broadcast_to(r, unit.shape)

    def do_v(slot):
        for h, at in both:
            vt[h, :, span(slot)] = vals(slot)[:, at].T

    dens = [jnp.zeros((1, TILE), F32), jnp.zeros((1, TILE), F32)]

    def score(slot):
        on = mask[slots[slot], 0, tile].astype(F32)
        for h, _ in both:
            e = jnp.exp2(dot(knorm[h, span(slot), :], qst[h])) * on
            dens[h] = dens[h] + jnp.sum(e, axis=0, keepdims=True)
            expo[h, span(slot), :] = e.astype(BF16)

    do_k(0)
    do_v(0)
    k_copies[0].wait_recv()
    do_k(1)
    k_copies[1].wait_recv()
    do_k(2)
    v_copies[0].wait_recv()
    do_v(1)
    v_copies[1].wait_recv()
    do_v(2)
    wait_in(2)
    for h, at in both:
        unit, r = norm(rx[2, :, at])
        qunit[h] = unit
        qrb[h] = jnp.broadcast_to(r, unit.shape)
        n = (unit * (g0 * (SCALE * LOG2E))).astype(BF16)
        qs[h] = n
        qst[h] = n.T
    for slot in range(3):
        score(slot)
    invs = [1.0 / dens[0], 1.0 / dens[1]]

    def send_out(i, first=1, end=heads):
        def block(n):
            return ob.at[i, rows(n), :], land.at[i, :, cols(chip)]

        def to(n):
            src, dst = block(n)
            remote(src, dst, out_send.at[i], out_recv.at[i], {"slab": tile, "head": n}).start()

        def step(s, carry):
            to(lax.rem(head + s * stride, heads))
            return carry

        lax.fori_loop(first, end, step, 0)
        if end == heads:

            @pl.when(core != side)
            def _():
                to(head)

            @pl.when(core == side)
            def _():
                src, dst = block(head)
                pltpu.make_async_copy(src, dst, out_recv.at[i]).start()

    outs = []
    for h, at in both:
        out_t = (dot(vt[h], expo[h]) * invs[h]).astype(BF16)
        ob[0, :, at] = out_t.T
        outs.append(out_t.astype(F32))
    send_out(0)

    def norm_backward(unit, r, gain, grad):
        inner = grad * gain
        return r * (inner - unit * jnp.mean(inner * unit, axis=-1, keepdims=True))

    douts = []
    doscs = []
    deltas = []

    def dscore(slot):
        for h, at in both:
            dp = dot(vals(slot)[:, at], douts[h])
            dsc[h, span(slot), :] = (expo[h, span(slot), :].astype(F32) * (dp - deltas[h])).astype(BF16)

    wait_in(3)
    for h, at in both:
        dt = rx[3, :, at].T.astype(F32) * invs[h]
        dtb = dt.astype(BF16)
        douts.append(dtb)
        deltas.append(jnp.sum(dtb.astype(F32) * outs[h], axis=0, keepdims=True))

    hg_copies = {}

    def send_near(i, n):
        hg_copies[i, n] = remote(hg_out.at[i, n], hg_in.at[i, n], hg_send.at[i, n], hg_recv.at[i, n], near[n])
        hg_copies[i, n].start()

    gain_k = jnp.zeros((1, HD), F32)
    gain_q = jnp.zeros((1, HD), F32)
    dks = []

    def do_dk(slot, total_k):
        for h, at in both:
            dk = dot(dsc[h, span(slot), :], qs[h]) * LN2
            total_k = total_k + jnp.sum(dk * kunit[h, span(slot), :], axis=0, keepdims=True)
            if slot > 0:
                hg_out[0, slot - 1, :, at] = dk.astype(BF16)
            else:
                dks.append(dk)
        if slot > 0:
            send_near(0, slot - 1)
        return total_k

    dscore(2)
    gain_k = do_dk(2, gain_k)
    dscore(1)
    dscore(0)
    for h, at in both:
        dq = dot(knt[h], dsc[h]).T * SCALE
        gain_q = gain_q + jnp.sum(dq * qunit[h], axis=0, keepdims=True)
        ob[1, :, at] = norm_backward(qunit[h], qrb[h], g0, dq).astype(BF16)
    send_out(1)
    gain_k = do_dk(1, gain_k)
    gain_k = do_dk(0, gain_k)

    stages = (
        (gring, me, ring, ring_id),
        (gz, plane, planes, plane_id),
        (gx, clip, clips, lambda x: {"dp": x}),
    )

    def gain_start(which, part):
        buf, here, count, target = stages[which]
        buf[here] = part

        def step(s, c):
            remote(
                buf.at[here], buf.at[here], g_send.at[which], g_recv.at[which], target(lax.rem(here + s, count))
            ).start()
            return c

        lax.fori_loop(1, count, step, 0)

    def gain_end(which):
        buf, _, count, _ = stages[which]
        if count > 1:
            wait_bytes(buf.at[pl.ds(0, count - 1)], g_recv.at[which])
        return jnp.sum(buf[...], axis=0)

    gain_start(0, jnp.concatenate([gain_q, gain_k, jnp.zeros((6, HD), F32)], axis=0))
    for h, at in both:
        doscs.append(douts[h].T)
    for n in (1, 0):
        for h, at in both:
            hg_out[1, n, :, at] = dot(expo[h, span(n + 1), :], doscs[h]).astype(BF16)
        send_near(1, n)
    hg_copies[0, 0].wait_recv()
    hg_copies[0, 1].wait_recv()
    for h, at in both:
        dk = dks[h] + hg_in[0, 0, :, at].astype(F32) + hg_in[0, 1, :, at].astype(F32)
        ob[3, :, at] = norm_backward(kunit[h, span(0), :], krb[h], g1, dk).astype(BF16)
    gain_start(1, gain_end(0))
    send_out(3)
    hg_copies[1, 0].wait_recv()
    hg_copies[1, 1].wait_recv()
    for h, at in both:
        dv = dot(expo[h, span(0), :], doscs[h])
        ob[2, :, at] = (dv + hg_in[1, 0, :, at].astype(F32) + hg_in[1, 1, :, at].astype(F32)).astype(BF16)
    send_out(2, 1, heads // 2)
    gain_start(2, gain_end(1))
    send_out(2, heads // 2, heads)
    gain_out[...] = gain_end(2)[0:2, :] * (1.0 / math.sqrt(total))

    def wait_sent(count):
        for i in range(4):
            wait_bytes(rx.at[i, pl.ds(0, count * chunk), :], in_send.at[i])
            wait_bytes(ob.at[i, pl.ds(0, count * chunk), :], out_send.at[i])

    for i in range(4):
        wait_bytes(ob.at[i], out_recv.at[i])
    for copy in k_copies + v_copies + list(hg_copies.values()):
        copy.wait_send()
    for which, (buf, _, count, _) in enumerate(stages):
        if count > 1:
            wait_bytes(buf.at[pl.ds(0, count - 1)], g_send.at[which])

    @pl.when(core == side)
    def _():
        wait_sent(heads - 1)

    @pl.when(core != side)
    def _():
        wait_sent(heads)


def store(land, gain, att, qg, vg, kg, gain_out, sems):
    copies = [pltpu.make_async_copy(gain, gain_out, sems.at[4])]
    for i, out in enumerate((att, qg, vg, kg)):
        copies.append(pltpu.make_async_copy(land.at[i], out.at[0], sems.at[i]))
    for copy in copies:
        copy.start()
    for copy in copies:
        copy.wait()


def solution(mesh):
    heads = mesh.shape["head"]
    planes = mesh.shape["slab"] // 2
    clips = mesh.shape["dp"]
    ring = 2 * heads
    chunk = TILE // heads
    total = clips * planes * 2 * TILE * ring
    sizes = (heads, planes, clips, total)

    def local(q_proj, k_proj, v_proj, grad_out, norm_gains, window_mask):
        hbm = pl.BlockSpec(memory_space=pltpu.HBM)
        vmem = pl.BlockSpec(memory_space=pltpu.VMEM)
        big = jax.ShapeDtypeStruct(q_proj.shape, BF16)
        sums = jax.ShapeDtypeStruct((2, HD), F32)
        dma = pltpu.SemaphoreType.DMA
        wide = 2 * HD
        landing = (pltpu.VMEM((4, chunk, ring * HD), BF16), pltpu.VMEM((2, HD), F32))
        operands = (q_proj, k_proj, v_proj, grad_out, norm_gains, jnp.transpose(window_mask, (2, 0, 1)))
        outs = pl.pallas_call(
            functools.partial(kernel, sizes),
            out_shape=landing,
            in_specs=[hbm] * 6,
            out_specs=(vmem,) * 2,
            scratch_shapes=[
                pltpu.VMEM((4, TILE, wide), BF16),
                pltpu.VMEM((2, TILE, wide), BF16),
                pltpu.VMEM((2, TILE, wide), BF16),
                pltpu.VMEM((2, 3 * TILE, HD), BF16),
                pltpu.VMEM((2, HD, 3 * TILE), BF16),
                pltpu.VMEM((2, HD, 3 * TILE), BF16),
                pltpu.VMEM((2, TILE, HD), BF16),
                pltpu.VMEM((2, HD, TILE), BF16),
                pltpu.VMEM((2, 3 * TILE, HD), F32),
                pltpu.VMEM((2, TILE, HD), F32),
                pltpu.VMEM((2, TILE, HD), F32),
                pltpu.VMEM((2, TILE, HD), F32),
                pltpu.VMEM((2, 3 * TILE, TILE), BF16),
                pltpu.VMEM((2, 3 * TILE, TILE), BF16),
                pltpu.VMEM((4, TILE, wide), BF16),
                pltpu.VMEM((2, 2, TILE, wide), BF16),
                pltpu.VMEM((2, 2, TILE, wide), BF16),
                pltpu.VMEM((ring, 8, HD), F32),
                pltpu.VMEM((planes, 8, HD), F32),
                pltpu.VMEM((clips, 8, HD), F32),
                pltpu.VMEM((2, HD), F32),
                pltpu.SMEM((3, 1, 2 * planes), jnp.int32),
                dma((2,)),
                dma((4,)),
                dma((4,)),
                dma((2, 2)),
                dma((2, 2)),
                dma((2, 2)),
                dma((2, 2)),
                dma((4,)),
                dma((4,)),
                dma((3,)),
                dma((3,)),
            ],
            compiler_params=pltpu.CompilerParams(
                collective_id=0, has_side_effects=True, vmem_limit_bytes=40 * 1024 * 1024
            ),
        )(*(pltpu.with_memory_space_constraint(x, pltpu.HBM) for x in operands))
        att, qg, vg, kg, gain = pl.pallas_call(
            store,
            out_shape=(big, big, big, big, sums),
            in_specs=[vmem] * 2,
            out_specs=(hbm,) * 5,
            scratch_shapes=[dma((5,))],
            compiler_params=pltpu.CompilerParams(vmem_limit_bytes=4 * 1024 * 1024),
        )(*(pltpu.with_memory_space_constraint(x, pltpu.VMEM) for x in outs))
        return att, qg, kg, vg, gain

    tokens = P("dp", ("slab", "head"), None)
    return jax.shard_map(
        local,
        mesh=mesh,
        in_specs=(tokens, tokens, tokens, tokens, P(), P("dp", None, None)),
        out_specs=(tokens, tokens, tokens, tokens, P()),
        check_vma=False,
    )
```

```python
import functools
import math

import jax
import jax.numpy as jnp
from jax import lax
from jax.experimental import pallas as pl
from jax.experimental.pallas import tpu as pltpu
from jax.sharding import PartitionSpec as P

MESH = pl.DeviceIdType.MESH
TILE = 384
HD = 128
EPS = 1e-06
SCALE = HD**-0.5
LOG2E = math.log2(math.e)
LN2 = math.log(2.0)
F32 = jnp.float32
BF16 = jnp.bfloat16


def dot(a, b, dims=((1,), (0,))):
    return lax.dot_general(a, b, (dims, ((), ())), preferred_element_type=F32)


def kernel(
    sizes,
    q_in, k_in, v_in, d_in, gains_in, mask_in,
    land, gain_out,
    rx, kh, vh,
    knorm, knt, vt, qs, qst,
    kunit, krb, qunit, qrb,
    expo, dsc, ob, hg_out, hg_in,
    gring, gz, gx, gains, mask,
    small_sem, in_send, in_recv, kv_send, kv_recv, hg_send, hg_recv, out_send, out_recv, g_send, g_recv,
):
    heads, planes, clips, total = sizes
    ring = 2 * heads
    chips = heads
    chunk = TILE // heads
    pair = 2 * HD
    slab = lax.axis_index("slab")
    head = lax.axis_index("head")
    clip = lax.axis_index("dp")
    plane = lax.div(slab, 2)
    side = lax.rem(slab, 2)
    core = lax.rem(head, 2)
    me = side * heads + head
    chip = lax.div(me, 2)
    tile = 2 * plane + core

    def ring_id(p):
        return {"slab": 2 * plane + lax.div(p, heads), "head": lax.rem(p, heads)}

    def plane_id(z):
        return {"slab": 2 * z + side}

    def rows(n):
        return pl.ds(pl.multiple_of(n * chunk, 16), chunk)

    def cols(c):
        return pl.ds(pl.multiple_of(c * pair, pair), pair)

    stride = 3 + 2 * core

    other = head + 1 - 2 * core
    next_plane = lax.rem(plane + planes - 1 + 2 * core, planes)
    near = ({"head": other}, {"slab": 2 * next_plane + side, "head": other})
    slots = (1, 2 - 2 * core, 2 * core)

    small = [
        pltpu.make_async_copy(gains_in, gains, small_sem.at[0]),
        pltpu.make_async_copy(mask_in, mask, small_sem.at[1]),
    ]
    for copy in small:
        copy.start()

    barrier = pltpu.get_barrier_semaphore()

    def greet(target):
        pl.semaphore_signal(barrier, inc=1, device_id=target, device_id_type=MESH)

    def greet_ring(s, c):
        greet(ring_id(lax.rem(me + s, ring)))
        return c

    def greet_plane(s, c):
        greet(plane_id(lax.rem(plane + s, planes)))
        return c

    def greet_clip(s, c):
        greet({"dp": lax.rem(clip + s, clips)})
        return c

    lax.fori_loop(1, ring, greet_ring, 0)
    greet(near[1])
    lax.fori_loop(1, planes, greet_plane, 0)
    lax.fori_loop(1, clips, greet_clip, 0)
    pl.semaphore_wait(barrier, ring + planes - 1 + clips - 1)

    def wait_bytes(ref, sem):
        pltpu.make_async_copy(ref, ref, sem).wait()

    def remote(src, dst, send_sem, recv_sem, target):
        return pltpu.make_async_remote_copy(
            src_ref=src,
            dst_ref=dst,
            send_sem=send_sem,
            recv_sem=recv_sem,
            device_id=target,
            device_id_type=MESH,
        )

    sources = (k_in, v_in, q_in, d_in)

    def send_in(i, first=1, end=chips):
        def block(c):
            return sources[i].at[0, :, cols(c)], rx.at[i, rows(head), :]

        def to(c):
            src, dst = block(c)
            remote(src, dst, in_send.at[i], in_recv.at[i], ring_id(2 * c + side)).start()

        def step(s, carry):
            to(lax.rem(chip + s * stride, chips))
            return carry

        lax.fori_loop(first, end, step, 0)
        if end == chips:

            @pl.when(core != side)
            def _():
                to(chip)

            @pl.when(core == side)
            def _():
                src, dst = block(chip)
                pltpu.make_async_copy(src, dst, in_recv.at[i]).start()

    def wait_in(i):
        wait_bytes(rx.at[i], in_recv.at[i])

    def near_copies(src, dst, send_sem, recv_sem, which=(1, 0)):
        copies = [None, None]
        for n in which:
            copies[n] = remote(src(n), dst(n), send_sem.at[n], recv_sem.at[n], near[n])
            copies[n].start()
        return copies

    send_in(0)
    send_in(1)
    wait_in(0)
    k_copies = near_copies(lambda n: rx.at[0], lambda n: kh.at[n], kv_send.at[0], kv_recv.at[0])
    send_in(2, 1, chips // 2)
    wait_in(1)
    v_copies = near_copies(lambda n: rx.at[1], lambda n: vh.at[n], kv_send.at[1], kv_recv.at[1])
    send_in(2, chips // 2, chips)
    send_in(3)
    for copy in small:
        copy.wait()

    g0 = gains[0:1, :]
    g1 = gains[1:2, :]
    both = tuple((h, slice(h * HD, (h + 1) * HD)) for h in (0, 1))

    def norm(raw):
        x = raw.astype(F32)
        r = lax.rsqrt(jnp.mean(x * x, axis=-1, keepdims=True) + EPS)
        return x * r, r

    def span(slot):
        return slice(slot * TILE, (slot + 1) * TILE)

    def keys(slot):
        return rx.at[0] if slot == 0 else kh.at[slot - 1]

    def vals(slot):
        return rx.at[1] if slot == 0 else vh.at[slot - 1]

    def do_k(slot):
        for h, at in both:
            unit, r = norm(keys(slot)[:, at])
            n = (unit * g1).astype(BF16)
            knorm[h, span(slot), :] = n
            knt[h, :, span(slot)] = n.T
            kunit[h, span(slot), :] = unit
            if slot == 0:
                krb[h] = jnp.broadcast_to(r, unit.shape)

    def do_v(slot):
        for h, at in both:
            vt[h, :, span(slot)] = vals(slot)[:, at].T

    dens = [jnp.zeros((1, TILE), F32), jnp.zeros((1, TILE), F32)]

    def score(slot):
        on = mask[slots[slot], 0, tile].astype(F32)
        for h, _ in both:
            e = jnp.exp2(dot(knorm[h, span(slot), :], qst[h])) * on
            dens[h] = dens[h] + jnp.sum(e, axis=0, keepdims=True)
            expo[h, span(slot), :] = e.astype(BF16)

    do_k(0)
    do_v(0)
    k_copies[0].wait_recv()
    do_k(1)
    k_copies[1].wait_recv()
    do_k(2)
    v_copies[0].wait_recv()
    do_v(1)
    v_copies[1].wait_recv()
    do_v(2)
    wait_in(2)
    for h, at in both:
        unit, r = norm(rx[2, :, at])
        qunit[h] = unit
        qrb[h] = jnp.broadcast_to(r, unit.shape)
        n = (unit * (g0 * (SCALE * LOG2E))).astype(BF16)
        qs[h] = n
        qst[h] = n.T
    for slot in range(3):
        score(slot)
    invs = [1.0 / dens[0], 1.0 / dens[1]]

    def send_out(i, first=1, end=heads):
        def block(n):
            return ob.at[i, rows(n), :], land.at[i, :, cols(chip)]

        def to(n):
            src, dst = block(n)
            remote(src, dst, out_send.at[i], out_recv.at[i], {"slab": tile, "head": n}).start()

        def step(s, carry):
            to(lax.rem(head + s * stride, heads))
            return carry

        lax.fori_loop(first, end, step, 0)
        if end == heads:

            @pl.when(core != side)
            def _():
                to(head)

            @pl.when(core == side)
            def _():
                src, dst = block(head)
                pltpu.make_async_copy(src, dst, out_recv.at[i]).start()

    outs = []
    for h, at in both:
        out_t = (dot(vt[h], expo[h]) * invs[h]).astype(BF16)
        ob[0, :, at] = out_t.T
        outs.append(out_t.astype(F32))
    send_out(0)

    def norm_backward(unit, r, gain, grad):
        inner = grad * gain
        return r * (inner - unit * jnp.mean(inner * unit, axis=-1, keepdims=True))

    douts = []
    doscs = []
    deltas = []

    def dscore(slot):
        for h, at in both:
            dp = dot(vals(slot)[:, at], douts[h])
            dsc[h, span(slot), :] = (expo[h, span(slot), :].astype(F32) * (dp - deltas[h])).astype(BF16)

    wait_in(3)
    for h, at in both:
        dt = rx[3, :, at].T.astype(F32) * invs[h]
        dtb = dt.astype(BF16)
        douts.append(dtb)
        deltas.append(jnp.sum(dtb.astype(F32) * outs[h], axis=0, keepdims=True))

    hg_copies = {}

    def send_near(i, n):
        hg_copies[i, n] = remote(hg_out.at[i, n], hg_in.at[i, n], hg_send.at[i, n], hg_recv.at[i, n], near[n])
        hg_copies[i, n].start()

    gain_k = jnp.zeros((1, HD), F32)
    dks = []
    for slot in (2, 1, 0):
        dscore(slot)
        for h, at in both:
            dk = dot(dsc[h, span(slot), :], qs[h]) * LN2
            gain_k = gain_k + jnp.sum(dk * kunit[h, span(slot), :], axis=0, keepdims=True)
            if slot > 0:
                hg_out[0, slot - 1, :, at] = dk.astype(BF16)
            else:
                dks.append(dk)
        if slot > 0:
            send_near(0, slot - 1)
    gain_q = jnp.zeros((1, HD), F32)
    dqs = []
    for h, at in both:
        dq = dot(knt[h], dsc[h]).T * SCALE
        gain_q = gain_q + jnp.sum(dq * qunit[h], axis=0, keepdims=True)
        dqs.append(dq)

    stages = (
        (gring, me, ring, ring_id),
        (gz, plane, planes, plane_id),
        (gx, clip, clips, lambda x: {"dp": x}),
    )

    def gain_start(which, part):
        buf, here, count, target = stages[which]
        buf[here] = part

        def step(s, c):
            remote(
                buf.at[here], buf.at[here], g_send.at[which], g_recv.at[which], target(lax.rem(here + s, count))
            ).start()
            return c

        lax.fori_loop(1, count, step, 0)

    def gain_end(which):
        buf, _, count, _ = stages[which]
        if count > 1:
            wait_bytes(buf.at[pl.ds(0, count - 1)], g_recv.at[which])
        return jnp.sum(buf[...], axis=0)

    gain_start(0, jnp.concatenate([gain_q, gain_k, jnp.zeros((6, HD), F32)], axis=0))
    for h, at in both:
        doscs.append(douts[h].T)
    for n in (1, 0):
        for h, at in both:
            hg_out[1, n, :, at] = dot(expo[h, span(n + 1), :], doscs[h]).astype(BF16)
        send_near(1, n)
    for h, at in both:
        ob[1, :, at] = norm_backward(qunit[h], qrb[h], g0, dqs[h]).astype(BF16)
    send_out(1)
    gain_start(1, gain_end(0))
    hg_copies[0, 0].wait_recv()
    hg_copies[0, 1].wait_recv()
    for h, at in both:
        dk = dks[h] + hg_in[0, 0, :, at].astype(F32) + hg_in[0, 1, :, at].astype(F32)
        ob[3, :, at] = norm_backward(kunit[h, span(0), :], krb[h], g1, dk).astype(BF16)
    send_out(3)
    hg_copies[1, 0].wait_recv()
    hg_copies[1, 1].wait_recv()
    for h, at in both:
        dv = dot(expo[h, span(0), :], doscs[h])
        ob[2, :, at] = (dv + hg_in[1, 0, :, at].astype(F32) + hg_in[1, 1, :, at].astype(F32)).astype(BF16)
    gain_start(2, gain_end(1))
    send_out(2)
    gain_out[...] = gain_end(2)[0:2, :] * (1.0 / math.sqrt(total))

    def wait_sent(count):
        for i in range(4):
            wait_bytes(rx.at[i, pl.ds(0, count * chunk), :], in_send.at[i])
            wait_bytes(ob.at[i, pl.ds(0, count * chunk), :], out_send.at[i])

    for i in range(4):
        wait_bytes(ob.at[i], out_recv.at[i])
    for copy in k_copies + v_copies + list(hg_copies.values()):
        copy.wait_send()
    for which, (buf, _, count, _) in enumerate(stages):
        if count > 1:
            wait_bytes(buf.at[pl.ds(0, count - 1)], g_send.at[which])

    @pl.when(core == side)
    def _():
        wait_sent(heads - 1)

    @pl.when(core != side)
    def _():
        wait_sent(heads)


def store(land, gain, att, qg, vg, kg, gain_out, sems):
    copies = [pltpu.make_async_copy(gain, gain_out, sems.at[4])]
    for i, out in enumerate((att, qg, vg, kg)):
        copies.append(pltpu.make_async_copy(land.at[i], out.at[0], sems.at[i]))
    for copy in copies:
        copy.start()
    for copy in copies:
        copy.wait()


def solution(mesh):
    heads = mesh.shape["head"]
    planes = mesh.shape["slab"] // 2
    clips = mesh.shape["dp"]
    ring = 2 * heads
    chunk = TILE // heads
    total = clips * planes * 2 * TILE * ring
    sizes = (heads, planes, clips, total)

    def local(q_proj, k_proj, v_proj, grad_out, norm_gains, window_mask):
        hbm = pl.BlockSpec(memory_space=pltpu.HBM)
        vmem = pl.BlockSpec(memory_space=pltpu.VMEM)
        big = jax.ShapeDtypeStruct(q_proj.shape, BF16)
        sums = jax.ShapeDtypeStruct((2, HD), F32)
        dma = pltpu.SemaphoreType.DMA
        wide = 2 * HD
        landing = (pltpu.VMEM((4, chunk, ring * HD), BF16), pltpu.VMEM((2, HD), F32))
        operands = (q_proj, k_proj, v_proj, grad_out, norm_gains, jnp.transpose(window_mask, (2, 0, 1)))
        outs = pl.pallas_call(
            functools.partial(kernel, sizes),
            out_shape=landing,
            in_specs=[hbm] * 6,
            out_specs=(vmem,) * 2,
            scratch_shapes=[
                pltpu.VMEM((4, TILE, wide), BF16),
                pltpu.VMEM((2, TILE, wide), BF16),
                pltpu.VMEM((2, TILE, wide), BF16),
                pltpu.VMEM((2, 3 * TILE, HD), BF16),
                pltpu.VMEM((2, HD, 3 * TILE), BF16),
                pltpu.VMEM((2, HD, 3 * TILE), BF16),
                pltpu.VMEM((2, TILE, HD), BF16),
                pltpu.VMEM((2, HD, TILE), BF16),
                pltpu.VMEM((2, 3 * TILE, HD), F32),
                pltpu.VMEM((2, TILE, HD), F32),
                pltpu.VMEM((2, TILE, HD), F32),
                pltpu.VMEM((2, TILE, HD), F32),
                pltpu.VMEM((2, 3 * TILE, TILE), BF16),
                pltpu.VMEM((2, 3 * TILE, TILE), BF16),
                pltpu.VMEM((4, TILE, wide), BF16),
                pltpu.VMEM((2, 2, TILE, wide), BF16),
                pltpu.VMEM((2, 2, TILE, wide), BF16),
                pltpu.VMEM((ring, 8, HD), F32),
                pltpu.VMEM((planes, 8, HD), F32),
                pltpu.VMEM((clips, 8, HD), F32),
                pltpu.VMEM((2, HD), F32),
                pltpu.SMEM((3, 1, 2 * planes), jnp.int32),
                dma((2,)),
                dma((4,)),
                dma((4,)),
                dma((2, 2)),
                dma((2, 2)),
                dma((2, 2)),
                dma((2, 2)),
                dma((4,)),
                dma((4,)),
                dma((3,)),
                dma((3,)),
            ],
            compiler_params=pltpu.CompilerParams(
                collective_id=0, has_side_effects=True, vmem_limit_bytes=40 * 1024 * 1024
            ),
        )(*(pltpu.with_memory_space_constraint(x, pltpu.HBM) for x in operands))
        att, qg, vg, kg, gain = pl.pallas_call(
            store,
            out_shape=(big, big, big, big, sums),
            in_specs=[vmem] * 2,
            out_specs=(hbm,) * 5,
            scratch_shapes=[dma((5,))],
            compiler_params=pltpu.CompilerParams(vmem_limit_bytes=4 * 1024 * 1024),
        )(*(pltpu.with_memory_space_constraint(x, pltpu.VMEM) for x in outs))
        return att, qg, kg, vg, gain

    tokens = P("dp", ("slab", "head"), None)
    return jax.shard_map(
        local,
        mesh=mesh,
        in_specs=(tokens, tokens, tokens, tokens, P(), P("dp", None, None)),
        out_specs=(tokens, tokens, tokens, tokens, P()),
        check_vma=False,
    )
```

```python
import functools
import math

import jax
import jax.numpy as jnp
from jax import lax
from jax.experimental import pallas as pl
from jax.experimental.pallas import tpu as pltpu
from jax.sharding import PartitionSpec as P

MESH = pl.DeviceIdType.MESH
TILE = 384
HD = 128
EPS = 1e-06
SCALE = HD**-0.5
LOG2E = math.log2(math.e)
LN2 = math.log(2.0)
F32 = jnp.float32
BF16 = jnp.bfloat16


def dot(a, b, dims=((1,), (0,))):
    return lax.dot_general(a, b, (dims, ((), ())), preferred_element_type=F32)


def kernel(
    sizes,
    q_in, k_in, v_in, d_in, gains_in, mask_in,
    land, gain_out,
    rx, kh, vh,
    knorm, knt, vt, qs, qst,
    kunit, krb, qunit, qrb,
    expo, dsc, ob, hg_out, hg_in,
    gring, gz, gx, gains, mask,
    small_sem, in_send, in_recv, kv_send, kv_recv, hg_send, hg_recv, out_send, out_recv, g_send, g_recv,
):
    heads, planes, clips, total = sizes
    ring = 2 * heads
    chips = heads
    chunk = TILE // heads
    pair = 2 * HD
    slab = lax.axis_index("slab")
    head = lax.axis_index("head")
    clip = lax.axis_index("dp")
    plane = lax.div(slab, 2)
    side = lax.rem(slab, 2)
    core = lax.rem(head, 2)
    me = side * heads + head
    chip = lax.div(me, 2)
    tile = 2 * plane + core

    def ring_id(p):
        return {"slab": 2 * plane + lax.div(p, heads), "head": lax.rem(p, heads)}

    def plane_id(z):
        return {"slab": 2 * z + side}

    def rows(n):
        return pl.ds(pl.multiple_of(n * chunk, 16), chunk)

    def cols(c):
        return pl.ds(pl.multiple_of(c * pair, pair), pair)

    stride = 3 + 2 * core

    other = head + 1 - 2 * core
    next_plane = lax.rem(plane + planes - 1 + 2 * core, planes)
    near = ({"head": other}, {"slab": 2 * next_plane + side, "head": other})
    slots = (1, 2 - 2 * core, 2 * core)

    small = [
        pltpu.make_async_copy(gains_in, gains, small_sem.at[0]),
        pltpu.make_async_copy(mask_in, mask, small_sem.at[1]),
    ]
    for copy in small:
        copy.start()

    barrier = pltpu.get_barrier_semaphore()

    def greet(target):
        pl.semaphore_signal(barrier, inc=1, device_id=target, device_id_type=MESH)

    def greet_ring(s, c):
        greet(ring_id(lax.rem(me + s, ring)))
        return c

    def greet_plane(s, c):
        greet(plane_id(lax.rem(plane + s, planes)))
        return c

    def greet_clip(s, c):
        greet({"dp": lax.rem(clip + s, clips)})
        return c

    lax.fori_loop(1, ring, greet_ring, 0)
    greet(near[1])
    lax.fori_loop(1, planes, greet_plane, 0)
    lax.fori_loop(1, clips, greet_clip, 0)
    pl.semaphore_wait(barrier, ring + planes - 1 + clips - 1)

    def wait_bytes(ref, sem):
        pltpu.make_async_copy(ref, ref, sem).wait()

    def remote(src, dst, send_sem, recv_sem, target):
        return pltpu.make_async_remote_copy(
            src_ref=src,
            dst_ref=dst,
            send_sem=send_sem,
            recv_sem=recv_sem,
            device_id=target,
            device_id_type=MESH,
        )

    sources = (k_in, v_in, q_in, d_in)

    def send_in(i, first=1, end=chips):
        def block(c):
            return sources[i].at[0, :, cols(c)], rx.at[i, rows(head), :]

        def to(c):
            src, dst = block(c)
            remote(src, dst, in_send.at[i], in_recv.at[i], ring_id(2 * c + side)).start()

        def step(s, carry):
            to(lax.rem(chip + s * stride, chips))
            return carry

        lax.fori_loop(first, end, step, 0)
        if end == chips:

            @pl.when(core != side)
            def _():
                to(chip)

            @pl.when(core == side)
            def _():
                src, dst = block(chip)
                pltpu.make_async_copy(src, dst, in_recv.at[i]).start()

    def wait_in(i):
        wait_bytes(rx.at[i], in_recv.at[i])

    def near_copies(src, dst, send_sem, recv_sem, which=(1, 0)):
        copies = [None, None]
        for n in which:
            copies[n] = remote(src(n), dst(n), send_sem.at[n], recv_sem.at[n], near[n])
            copies[n].start()
        return copies

    send_in(0)
    send_in(1)
    wait_in(0)
    k_copies = near_copies(lambda n: rx.at[0], lambda n: kh.at[n], kv_send.at[0], kv_recv.at[0])
    send_in(2, 1, chips // 2)
    wait_in(1)
    v_copies = near_copies(lambda n: rx.at[1], lambda n: vh.at[n], kv_send.at[1], kv_recv.at[1])
    send_in(2, chips // 2, chips)
    send_in(3)
    for copy in small:
        copy.wait()

    g0 = gains[0:1, :]
    g1 = gains[1:2, :]
    both = tuple((h, slice(h * HD, (h + 1) * HD)) for h in (0, 1))

    def norm(raw):
        x = raw.astype(F32)
        r = lax.rsqrt(jnp.mean(x * x, axis=-1, keepdims=True) + EPS)
        return x * r, r

    def span(slot):
        return slice(slot * TILE, (slot + 1) * TILE)

    def keys(slot):
        return rx.at[0] if slot == 0 else kh.at[slot - 1]

    def vals(slot):
        return rx.at[1] if slot == 0 else vh.at[slot - 1]

    def do_k(slot):
        for h, at in both:
            unit, r = norm(keys(slot)[:, at])
            n = (unit * g1).astype(BF16)
            knorm[h, span(slot), :] = n
            knt[h, :, span(slot)] = n.T
            kunit[h, span(slot), :] = unit
            if slot == 0:
                krb[h] = jnp.broadcast_to(r, unit.shape)

    def do_v(slot):
        for h, at in both:
            vt[h, :, span(slot)] = vals(slot)[:, at].T

    dens = [jnp.zeros((1, TILE), F32), jnp.zeros((1, TILE), F32)]

    def score(slot):
        on = mask[slots[slot], 0, tile].astype(F32)
        for h, _ in both:
            e = jnp.exp2(dot(knorm[h, span(slot), :], qst[h])) * on
            dens[h] = dens[h] + jnp.sum(e, axis=0, keepdims=True)
            expo[h, span(slot), :] = e.astype(BF16)

    do_k(0)
    do_v(0)
    k_copies[0].wait_recv()
    do_k(1)
    k_copies[1].wait_recv()
    do_k(2)
    v_copies[0].wait_recv()
    do_v(1)
    v_copies[1].wait_recv()
    do_v(2)
    wait_in(2)
    for h, at in both:
        unit, r = norm(rx[2, :, at])
        qunit[h] = unit
        qrb[h] = jnp.broadcast_to(r, unit.shape)
        n = (unit * (g0 * (SCALE * LOG2E))).astype(BF16)
        qs[h] = n
        qst[h] = n.T
    for slot in range(3):
        score(slot)
    invs = [1.0 / dens[0], 1.0 / dens[1]]

    def send_out(i, first=1, end=heads):
        def block(n):
            return ob.at[i, rows(n), :], land.at[i, :, cols(chip)]

        def to(n):
            src, dst = block(n)
            remote(src, dst, out_send.at[i], out_recv.at[i], {"slab": tile, "head": n}).start()

        def step(s, carry):
            to(lax.rem(head + s * stride, heads))
            return carry

        lax.fori_loop(first, end, step, 0)
        if end == heads:

            @pl.when(core != side)
            def _():
                to(head)

            @pl.when(core == side)
            def _():
                src, dst = block(head)
                pltpu.make_async_copy(src, dst, out_recv.at[i]).start()

    outs = []
    for h, at in both:
        out_t = (dot(vt[h], expo[h]) * invs[h]).astype(BF16)
        ob[0, :, at] = out_t.T
        outs.append(out_t.astype(F32))
    send_out(0)

    def norm_backward(unit, r, gain, grad):
        inner = grad * gain
        return r * (inner - unit * jnp.mean(inner * unit, axis=-1, keepdims=True))

    douts = []
    doscs = []
    deltas = []

    def dscore(slot):
        for h, at in both:
            dp = dot(vals(slot)[:, at], douts[h])
            dsc[h, span(slot), :] = (expo[h, span(slot), :].astype(F32) * (dp - deltas[h])).astype(BF16)

    wait_in(3)
    for h, at in both:
        dt = rx[3, :, at].T.astype(F32) * invs[h]
        dtb = dt.astype(BF16)
        douts.append(dtb)
        deltas.append(jnp.sum(dtb.astype(F32) * outs[h], axis=0, keepdims=True))

    hg_copies = {}

    def send_near(i, n):
        hg_copies[i, n] = remote(hg_out.at[i, n], hg_in.at[i, n], hg_send.at[i, n], hg_recv.at[i, n], near[n])
        hg_copies[i, n].start()

    gain_k = jnp.zeros((1, HD), F32)
    dks = []
    for slot in (2, 1, 0):
        dscore(slot)
        for h, at in both:
            dk = dot(dsc[h, span(slot), :], qs[h]) * LN2
            gain_k = gain_k + jnp.sum(dk * kunit[h, span(slot), :], axis=0, keepdims=True)
            if slot > 0:
                hg_out[0, slot - 1, :, at] = dk.astype(BF16)
            else:
                dks.append(dk)
        if slot > 0:
            send_near(0, slot - 1)
    gain_q = jnp.zeros((1, HD), F32)
    dqs = []
    for h, at in both:
        dq = dot(knt[h], dsc[h]).T * SCALE
        gain_q = gain_q + jnp.sum(dq * qunit[h], axis=0, keepdims=True)
        dqs.append(dq)

    stages = (
        (gring, me, ring, ring_id),
        (gz, plane, planes, plane_id),
        (gx, clip, clips, lambda x: {"dp": x}),
    )

    def gain_start(which, part):
        buf, here, count, target = stages[which]
        buf[here] = part

        def step(s, c):
            remote(
                buf.at[here], buf.at[here], g_send.at[which], g_recv.at[which], target(lax.rem(here + s, count))
            ).start()
            return c

        lax.fori_loop(1, count, step, 0)

    def gain_end(which):
        buf, _, count, _ = stages[which]
        if count > 1:
            wait_bytes(buf.at[pl.ds(0, count - 1)], g_recv.at[which])
        return jnp.sum(buf[...], axis=0)

    gain_start(0, jnp.concatenate([gain_q, gain_k, jnp.zeros((6, HD), F32)], axis=0))
    for h, at in both:
        doscs.append(douts[h].T)
    for n in (1, 0):
        for h, at in both:
            hg_out[1, n, :, at] = dot(expo[h, span(n + 1), :], doscs[h]).astype(BF16)
        send_near(1, n)
    for h, at in both:
        ob[1, :, at] = norm_backward(qunit[h], qrb[h], g0, dqs[h]).astype(BF16)
    send_out(1)
    hg_copies[0, 0].wait_recv()
    hg_copies[0, 1].wait_recv()
    for h, at in both:
        dk = dks[h] + hg_in[0, 0, :, at].astype(F32) + hg_in[0, 1, :, at].astype(F32)
        ob[3, :, at] = norm_backward(kunit[h, span(0), :], krb[h], g1, dk).astype(BF16)
    send_out(3)
    gain_start(1, gain_end(0))
    hg_copies[1, 0].wait_recv()
    hg_copies[1, 1].wait_recv()
    for h, at in both:
        dv = dot(expo[h, span(0), :], doscs[h])
        ob[2, :, at] = (dv + hg_in[1, 0, :, at].astype(F32) + hg_in[1, 1, :, at].astype(F32)).astype(BF16)
    send_out(2)
    gain_start(2, gain_end(1))
    gain_out[...] = gain_end(2)[0:2, :] * (1.0 / math.sqrt(total))

    def wait_sent(count):
        for i in range(4):
            wait_bytes(rx.at[i, pl.ds(0, count * chunk), :], in_send.at[i])
            wait_bytes(ob.at[i, pl.ds(0, count * chunk), :], out_send.at[i])

    for i in range(4):
        wait_bytes(ob.at[i], out_recv.at[i])
    for copy in k_copies + v_copies + list(hg_copies.values()):
        copy.wait_send()
    for which, (buf, _, count, _) in enumerate(stages):
        if count > 1:
            wait_bytes(buf.at[pl.ds(0, count - 1)], g_send.at[which])

    @pl.when(core == side)
    def _():
        wait_sent(heads - 1)

    @pl.when(core != side)
    def _():
        wait_sent(heads)


def store(land, gain, att, qg, vg, kg, gain_out, sems):
    copies = [pltpu.make_async_copy(gain, gain_out, sems.at[4])]
    for i, out in enumerate((att, qg, vg, kg)):
        copies.append(pltpu.make_async_copy(land.at[i], out.at[0], sems.at[i]))
    for copy in copies:
        copy.start()
    for copy in copies:
        copy.wait()


def solution(mesh):
    heads = mesh.shape["head"]
    planes = mesh.shape["slab"] // 2
    clips = mesh.shape["dp"]
    ring = 2 * heads
    chunk = TILE // heads
    total = clips * planes * 2 * TILE * ring
    sizes = (heads, planes, clips, total)

    def local(q_proj, k_proj, v_proj, grad_out, norm_gains, window_mask):
        hbm = pl.BlockSpec(memory_space=pltpu.HBM)
        vmem = pl.BlockSpec(memory_space=pltpu.VMEM)
        big = jax.ShapeDtypeStruct(q_proj.shape, BF16)
        sums = jax.ShapeDtypeStruct((2, HD), F32)
        dma = pltpu.SemaphoreType.DMA
        wide = 2 * HD
        landing = (pltpu.VMEM((4, chunk, ring * HD), BF16), pltpu.VMEM((2, HD), F32))
        operands = (q_proj, k_proj, v_proj, grad_out, norm_gains, jnp.transpose(window_mask, (2, 0, 1)))
        outs = pl.pallas_call(
            functools.partial(kernel, sizes),
            out_shape=landing,
            in_specs=[hbm] * 6,
            out_specs=(vmem,) * 2,
            scratch_shapes=[
                pltpu.VMEM((4, TILE, wide), BF16),
                pltpu.VMEM((2, TILE, wide), BF16),
                pltpu.VMEM((2, TILE, wide), BF16),
                pltpu.VMEM((2, 3 * TILE, HD), BF16),
                pltpu.VMEM((2, HD, 3 * TILE), BF16),
                pltpu.VMEM((2, HD, 3 * TILE), BF16),
                pltpu.VMEM((2, TILE, HD), BF16),
                pltpu.VMEM((2, HD, TILE), BF16),
                pltpu.VMEM((2, 3 * TILE, HD), F32),
                pltpu.VMEM((2, TILE, HD), F32),
                pltpu.VMEM((2, TILE, HD), F32),
                pltpu.VMEM((2, TILE, HD), F32),
                pltpu.VMEM((2, 3 * TILE, TILE), BF16),
                pltpu.VMEM((2, 3 * TILE, TILE), BF16),
                pltpu.VMEM((4, TILE, wide), BF16),
                pltpu.VMEM((2, 2, TILE, wide), BF16),
                pltpu.VMEM((2, 2, TILE, wide), BF16),
                pltpu.VMEM((ring, 8, HD), F32),
                pltpu.VMEM((planes, 8, HD), F32),
                pltpu.VMEM((clips, 8, HD), F32),
                pltpu.VMEM((2, HD), F32),
                pltpu.SMEM((3, 1, 2 * planes), jnp.int32),
                dma((2,)),
                dma((4,)),
                dma((4,)),
                dma((2, 2)),
                dma((2, 2)),
                dma((2, 2)),
                dma((2, 2)),
                dma((4,)),
                dma((4,)),
                dma((3,)),
                dma((3,)),
            ],
            compiler_params=pltpu.CompilerParams(
                collective_id=0, has_side_effects=True, vmem_limit_bytes=40 * 1024 * 1024
            ),
        )(*(pltpu.with_memory_space_constraint(x, pltpu.HBM) for x in operands))
        att, qg, vg, kg, gain = pl.pallas_call(
            store,
            out_shape=(big, big, big, big, sums),
            in_specs=[vmem] * 2,
            out_specs=(hbm,) * 5,
            scratch_shapes=[dma((5,))],
            compiler_params=pltpu.CompilerParams(vmem_limit_bytes=4 * 1024 * 1024),
        )(*(pltpu.with_memory_space_constraint(x, pltpu.VMEM) for x in outs))
        return att, qg, kg, vg, gain

    tokens = P("dp", ("slab", "head"), None)
    return jax.shard_map(
        local,
        mesh=mesh,
        in_specs=(tokens, tokens, tokens, tokens, P(), P("dp", None, None)),
        out_specs=(tokens, tokens, tokens, tokens, P()),
        check_vma=False,
    )
```
